32 devices in a mesh: rows: 8 (over y, x, core), cols: 4 (over z).
Axes of the slice: x: 2, y: 2, z: 4, core: 2. Of those that a mesh axis runs over, the one named last changes fastest.
Arguments:
- spectrum: bfloat16 [2, 4096, 4096], P(None, 'rows', 'cols'), may hold values from -6 to 6
- diffraction: bfloat16 [2, 32, 3, 128, 128], P(None, 'rows'), may hold values from -0.21875 to 0.21875
- order_mask: int32 [32, 3], P('rows'), may hold values from 0 to 1, as said below
- phases: float32 [2, 4096, 4096], P(None, 'rows', 'cols'), may hold values from -3.140625 to 3.140625
- transmission: float32 [4096, 4096], P('rows', 'cols'), may hold values from 0.2 to 1
- shifts: int32 [2], replicated, may hold values from 256 to 512, as said below
Outputs:
- outgoing: float32 [2, 4096, 4096], P(None, 'rows', 'cols')
The draws below stay inside these ranges and needn't reach their ends.
Inputs may be any that keep to these rules, and one draw needn't show every extreme that they name: Each bounce's shift lies between 256 and 512; one bounce shifts by exactly 512. `order_mask`: every block carries the orders -1 and +1; the order 0 is off in some blocks.
All inputs are finite; a program needn't handle non-finite values.
Results may differ from the reference program's by a relative error of at most 0.018.
Values may be sent and summed in bfloat16 or wider, within the bound.
No kernel may reach another device: no remote copies, remote signals or barrier semaphores. Data moves between devices by JAX's collectives and lax.ppermute only.
A program may use at most 192 MiB of HBM per device.

```python
import math
import jax
import jax.numpy as jnp
from jax import lax

NX = 4096
NY = 4096
BLOCK = 128
BASE = 256
BOUNCES = 2
NBLK = 32
GMAX = 512


def draw_shifts(key, part):
    first_key = jax.random.fold_in(key, 11)
    second_key = jax.random.fold_in(key, 23)
    drawn = jax.random.randint(first_key, (BOUNCES,), GMAX // 2, GMAX + 1)
    chosen = jax.random.randint(second_key, (), 0, BOUNCES)
    return jnp.where(jnp.arange(BOUNCES) == chosen, GMAX, drawn).astype(jnp.int32)


def draw_order_mask(key, part):
    first_key = jax.random.fold_in(key, 37)
    second_key = jax.random.fold_in(key, 41)
    middle = jax.random.randint(first_key, (NBLK,), 0, 2)
    chosen = jax.random.randint(second_key, (), 0, NBLK)
    middle = jnp.where(jnp.arange(NBLK) == chosen, 0, middle)
    sides = jnp.ones((NBLK,), jnp.int32)
    return jnp.stack([sides, middle, sides], axis=1).astype(jnp.int32)


def block_levels(own_key, shape, cuts, least, top_value):
    factor_of, own = 1.0, jax.random.fold_in(own_key, 6)
    for dim, blocks in cuts:
        steps = jnp.exp(jax.random.uniform(jax.random.fold_in(own, dim), (blocks,), jnp.float32, least / len(cuts), top_value / len(cuts)))
        factor_of = factor_of * jnp.repeat(steps, shape[dim] // blocks).reshape([-1 if axis == dim else 1 for axis in range(len(shape))])
    return factor_of


def normal_values(stream_key, dims, spread, most, split=(), kind=jnp.bfloat16):
    values = jax.random.normal(stream_key, dims, jnp.float32) * spread
    if len(split) > 0:
        values = block_levels(stream_key, dims, split, -0.22, 0.18) * values
    return jnp.clip(values, min=-most, max=most).astype(kind)


def setup_inputs(seed: int = 0) -> dict:
    key_list = jax.random.split(jax.random.key(seed), 7)
    spectrum = normal_values(key_list[0], (2, NX, NY), 1.0, 6.0, ((1, 8), (2, 4)))
    diffraction = normal_values(key_list[1], (2, NBLK, 3, BLOCK, BLOCK), (6 * BLOCK) ** -0.5, 0.21875, ((1, 8),))
    order_mask = draw_order_mask(jax.random.fold_in(key_list[6], 71), 0)
    phases = jnp.clip(jax.random.uniform(key_list[3], (BOUNCES, NX, NY), jnp.float32, -3.140625, 3.140625), -3.140625, 3.140625)
    transmission = jnp.clip(0.2 + 0.8 * jax.random.uniform(key_list[4], (NX, NY), jnp.float32) ** block_levels(key_list[4], (NX, NY), ((0, 8), (1, 4)), -0.2, 0.2), 0.2, 1.0)
    shifts = draw_shifts(jax.random.fold_in(key_list[6], 71), 0)
    return dict(spectrum=spectrum, diffraction=diffraction, order_mask=order_mask, phases=phases, transmission=transmission, shifts=shifts)


def rounded(values):
    return lax.optimization_barrier(values.astype(jnp.bfloat16))

def twiddles(extent, sign_value, left_index, right_index):
    wrapped = left_index[:, None] * right_index[None, :] % extent
    angles = wrapped.astype(jnp.float32) * (2.0 * math.pi / extent)
    return (jnp.cos(angles), sign_value * jnp.sin(angles))

def product(left_side, right_side):
    return jnp.dot(left_side, right_side, precision=lax.Precision.HIGHEST, preferred_element_type=jnp.float32)

def transform_first(values, sign_value):
    extent = values.shape[1]
    others = values.shape[2]
    target = jnp.arange(extent, dtype=jnp.int32)
    base_real, base_imag = twiddles(extent, sign_value, jnp.arange(BASE, dtype=jnp.int32), target)
    factor = 1.0 / math.sqrt(extent)
    base_real = rounded(base_real * factor).astype(jnp.float32).T
    base_imag = rounded(base_imag * factor).astype(jnp.float32).T
    blocked = values.astype(jnp.float32).reshape(2, extent // BASE, BASE, others).transpose(1, 0, 2, 3)

    def advance(running, element):
        number, segment = element
        inner_real = product(base_real, segment[0]) - product(base_imag, segment[1])
        inner_imag = product(base_imag, segment[0]) + product(base_real, segment[1])
        turn_real, turn_imag = twiddles(extent, sign_value, (number * BASE)[None], target)
        turn_real = turn_real[0][:, None]
        turn_imag = turn_imag[0][:, None]
        next_real = running[0] + turn_real * inner_real - turn_imag * inner_imag
        next_imag = running[1] + turn_real * inner_imag + turn_imag * inner_real
        return ((next_real, next_imag), number)
    initial = (jnp.zeros((extent, others), jnp.float32), jnp.zeros((extent, others), jnp.float32))
    numbers = jnp.arange(extent // BASE, dtype=jnp.int32)
    finished, ignored = lax.scan(advance, initial, (numbers, blocked))
    return jnp.stack([finished[0], finished[1]])

def transform_second(values, sign_value):
    return jnp.swapaxes(transform_first(jnp.swapaxes(values, 1, 2), sign_value), 1, 2)

def apply_blocks(left_side, right_side):
    return jnp.einsum('bjk,bkq->bjq', left_side, right_side, precision=lax.Precision.HIGHEST, preferred_element_type=jnp.float32)

def diffract(current, matrices, weights, offset_step):
    padded = jnp.pad(current, ((0, 0), (NX, NX), (0, 0)))
    result_real = jnp.zeros((NBLK, BLOCK, NY), jnp.float32)
    result_imag = jnp.zeros((NBLK, BLOCK, NY), jnp.float32)
    for order_at in range(3):
        start_row = NX + (order_at - 1) * offset_step
        source = lax.dynamic_slice_in_dim(padded, start_row, NX, 1).astype(jnp.float32).reshape(2, NBLK, BLOCK, NY)
        kernel = matrices[:, :, order_at].astype(jnp.float32)
        weight_now = weights[:, order_at][:, None, None]
        result_real = result_real + weight_now * (apply_blocks(kernel[0], source[0]) - apply_blocks(kernel[1], source[1]))
        result_imag = result_imag + weight_now * (apply_blocks(kernel[0], source[1]) + apply_blocks(kernel[1], source[0]))
    return (result_real.reshape(NX, NY), result_imag.reshape(NX, NY))

def reference(spectrum, diffraction, order_mask, phases, transmission, shifts):
    weights = order_mask.astype(jnp.float32)
    current = spectrum
    outgoing = None
    for bounce in range(BOUNCES):
        diff_real, diff_imag = diffract(current, diffraction, weights, shifts[bounce])
        cosine = jnp.cos(phases[bounce])
        sine_part = jnp.sin(phases[bounce])
        wave_k = rounded(jnp.stack([diff_real * cosine - diff_imag * sine_part, diff_real * sine_part + diff_imag * cosine]))
        rows_space = rounded(transform_first(wave_k, 1.0))
        space = transform_second(rows_space, 1.0) * transmission[None]
        if bounce == BOUNCES - 1:
            outgoing = space
        else:
            columns_k = rounded(transform_second(rounded(space), -1.0))
            current = rounded(transform_first(columns_k, -1.0))
    return outgoing
```

```python
import math

import jax
import jax.numpy as jnp
import ml_dtypes
import numpy as np
from jax import lax
from jax.experimental import pallas as pl
from jax.experimental.pallas import tpu as pltpu
from jax.sharding import PartitionSpec as P

BLOCK = 128
LANES = 128
RADIX = 16
BOUNCES = 2
VMEM_LIMIT = 56 * 1024 * 1024
BF16 = jnp.bfloat16
F32 = jnp.float32


def params():
    return pltpu.CompilerParams(vmem_limit_bytes=VMEM_LIMIT)


def vmem(count):
    return [pl.BlockSpec(memory_space=pltpu.VMEM) for _ in range(count)]


def column_tables(extent):
    part = extent // RADIX
    first = np.arange(RADIX)[:, None, None]
    second = np.arange(part)[None, :, None]
    inner = np.arange(part)[None, None, :]
    angle = ((first + RADIX * second) * inner % extent) * (2.0 * np.pi / extent)
    scale = 1.0 / math.sqrt(extent)
    real, imag = np.cos(angle) * scale, np.sin(angle) * scale
    forward = np.concatenate([real, imag], axis=1)
    backward = np.concatenate([real.transpose(0, 2, 1), imag.transpose(0, 2, 1)], axis=1)
    return forward.astype(ml_dtypes.bfloat16), backward.astype(ml_dtypes.bfloat16)


def row_tables(extent, part):
    radix = extent // part
    inner = np.arange(part)
    angle = (inner[:, None] * inner[None, :] % part) * (2.0 * np.pi / part)
    scale = 1.0 / math.sqrt(extent)
    core = np.concatenate([np.cos(angle) * scale, np.sin(angle) * scale], axis=1)
    turn = (np.arange(radix)[:, None] * inner[None, :]) * (2.0 * np.pi / extent)
    turns = np.stack([np.cos(turn), np.sin(turn)], axis=1)[:, :, None, :]
    return core.astype(ml_dtypes.bfloat16), turns.astype(np.float32)


def regroup(count, fast):
    natural = np.arange(count)
    grouped = (natural % fast) * (count // fast) + natural // fast
    matrix = np.zeros((count, count), np.float32)
    matrix[natural, grouped] = 1.0
    return matrix.astype(ml_dtypes.bfloat16)


def angle_series():
    squares = np.polynomial.chebyshev.chebpts1(200) * (np.pi**2 / 2) + np.pi**2 / 2
    angles = np.sqrt(squares)

    def fit(values, degree):
        series = np.polynomial.chebyshev.Chebyshev.fit(squares, values, degree, domain=[0, np.pi**2])
        return [float(c) for c in series.convert(kind=np.polynomial.Polynomial).coef]

    return fit(np.sin(angles) / angles, 7), fit(np.cos(angles), 8)


SINE_SERIES, COSINE_SERIES = angle_series()


def cos_sin(angle):
    square = angle * angle

    def series(coefs):
        total = jnp.full_like(square, coefs[-1])
        for coef in coefs[-2::-1]:
            total = total * square + coef
        return total

    return series(COSINE_SERIES), angle * series(SINE_SERIES)


def butterfly(values, sign):
    count = len(values)
    if count == 1:
        return values
    even, odd = butterfly(values[0::2], sign), butterfly(values[1::2], sign)
    low, high = [], []
    for at in range(count // 2):
        real, imag = odd[at]
        if at == 0:
            turned = real, imag
        elif 4 * at == count:
            turned = (-imag, real) if sign > 0 else (imag, -real)
        elif 8 * at == count:
            half = math.sqrt(0.5)
            turned = (
                ((real - imag) * half, (real + imag) * half)
                if sign > 0
                else ((real + imag) * half, (imag - real) * half)
            )
        elif 8 * at == 3 * count:
            half = math.sqrt(0.5)
            turned = (
                ((real + imag) * -half, (real - imag) * half)
                if sign > 0
                else ((imag - real) * half, (real + imag) * -half)
            )
        else:
            cosine = math.cos(2 * math.pi * at / count)
            sine = sign * math.sin(2 * math.pi * at / count)
            turned = real * cosine - imag * sine, real * sine + imag * cosine
        low.append((even[at][0] + turned[0], even[at][1] + turned[1]))
        high.append((even[at][0] - turned[0], even[at][1] - turned[1]))
    return low + high


def dot(left, right):
    return jnp.dot(left, right, preferred_element_type=F32)


def loop(count, body):
    def step(at, carry):
        body(at)
        return carry

    lax.fori_loop(0, count, step, 0)


def column_body(later, cur_ref, mats_ref, mask_ref, shift_ref, phase_ref, forward_ref, backward_ref, out_ref, padded, wave, mixed):
    rows_at, cols_at, firsts, _, seconds, width = out_ref.shape
    block_rows = mats_ref.shape[2]
    extent = wave.shape[1]
    part = extent // RADIX
    height = (padded.shape[1] - extent) // 2
    blocks = extent // BLOCK
    padded[:, pl.ds(0, height)] = jnp.zeros((2, height, width), F32)
    padded[:, pl.ds(height + extent, height)] = jnp.zeros((2, height, width), F32)

    if later:

        def unfold(at):
            group, first = at // firsts, at % firsts
            real = cur_ref[:, group, first, 0].reshape(part, width)
            imag = cur_ref[:, group, first, 1].reshape(part, width)
            got = dot(backward_ref[at], jnp.concatenate([real, imag], axis=1))
            wave[0, pl.ds(at * part, part)] = got[:part, :width] + got[part:, width:]
            wave[1, pl.ds(at * part, part)] = got[:part, width:] - got[part:, :width]

        loop(RADIX, unfold)

        def gather(at):
            rows = at * 16
            values = [
                (wave[0, pl.ds(one * part + rows, 16)], wave[1, pl.ds(one * part + rows, 16)])
                for one in range(RADIX)
            ]
            for one, (real, imag) in enumerate(butterfly(values, -1)):
                padded[0, pl.ds(height + one * part + rows, 16)] = real
                padded[1, pl.ds(height + one * part + rows, 16)] = imag

        loop(part // 16, gather)
    else:

        def spread(at):
            rows = pl.ds(height + at * height, height)
            padded[0, rows] = cur_ref[at, 0].astype(F32)
            padded[1, rows] = cur_ref[at, 1].astype(F32)

        loop(extent // height, spread)

    shift = shift_ref[0]

    def diffract(at):
        owner, inner = at // block_rows, at % block_rows
        lefts, rights = [], []
        for order in range(3):
            rows = pl.ds(height + at * BLOCK + (order - 1) * shift, BLOCK)
            rights.append(jnp.concatenate([padded[0, rows], padded[1, rows]], axis=1).astype(BF16))
            weight = mask_ref[at * 3 + order].astype(F32)
            lefts.append(
                jnp.concatenate([mats_ref[owner, 0, inner, order], mats_ref[owner, 1, inner, order]], axis=0)
                * weight.astype(BF16)
            )
        got = dot(jnp.concatenate(lefts, axis=1), jnp.concatenate(rights, axis=0))
        real = got[:BLOCK, :width] - got[BLOCK:, width:]
        imag = got[:BLOCK, width:] + got[BLOCK:, :width]
        rows = pl.ds(pl.multiple_of(at * BLOCK, BLOCK), BLOCK)
        cosine, sine = cos_sin(phase_ref[rows])
        wave[0, rows] = real * cosine - imag * sine
        wave[1, rows] = real * sine + imag * cosine

    loop(blocks, diffract)

    def mix(at):
        rows = at * 16
        values = [
            (wave[0, pl.ds(one * part + rows, 16)], wave[1, pl.ds(one * part + rows, 16)]) for one in range(RADIX)
        ]
        for one, (real, imag) in enumerate(butterfly(values, 1)):
            mixed[one, pl.ds(pl.multiple_of(rows, 16), 16)] = jnp.concatenate([real, imag], axis=1).astype(BF16)

    loop(part // 16, mix)

    def fold(at):
        group, first = at // firsts, at % firsts
        got = dot(forward_ref[at], mixed[at])
        real = (got[:part, :width] - got[part:, width:]).astype(BF16)
        imag = (got[:part, width:] + got[part:, :width]).astype(BF16)
        out_ref[:, group, first, 0] = real.reshape(rows_at, seconds, width)
        out_ref[:, group, first, 1] = imag.reshape(rows_at, seconds, width)

    loop(RADIX, fold)


def column_work(later, current, mats, mask, shift, phase, tables, row_count, col_count):
    extent, width = phase.shape
    part = extent // RADIX
    height = extent // row_count

    def body(*refs):
        column_body(later, *refs)

    in_specs = vmem(7)
    in_specs[2] = pl.BlockSpec(memory_space=pltpu.SMEM)
    in_specs[3] = pl.BlockSpec(memory_space=pltpu.SMEM)
    return pl.pallas_call(
        body,
        out_shape=jax.ShapeDtypeStruct(
            (row_count, col_count, RADIX // col_count, 2, part // row_count, width), BF16
        ),
        in_specs=in_specs,
        out_specs=vmem(1)[0],
        scratch_shapes=[
            pltpu.VMEM((2, extent + 2 * height, width), F32),
            pltpu.VMEM((2, extent, width), F32),
            pltpu.VMEM((RADIX, part, 2 * width), BF16),
        ],
        compiler_params=params(),
        name="column_later" if later else "column_first",
    )(current, mats, mask, shift, phase, *tables)


def row_mix(order, in_ref, turn_ref, mixed):
    blocks, firsts, _, seconds, lanes = in_ref.shape
    radix, _, part = mixed.shape
    tiles = part // lanes
    rows = firsts * seconds

    def one_first(first):
        for tile in range(tiles):
            across = pl.ds(tile * lanes, lanes)
            for at in range(0, seconds, 16):
                values = [
                    (
                        in_ref[order[one * tiles + tile], first, 0, pl.ds(at, 16)].astype(F32),
                        in_ref[order[one * tiles + tile], first, 1, pl.ds(at, 16)].astype(F32),
                    )
                    for one in range(radix)
                ]
                for one, (real, imag) in enumerate(butterfly(values, 1)):
                    cosine, sine = turn_ref[one, 0, :, across], turn_ref[one, 1, :, across]
                    down = pl.multiple_of(first * seconds + at, 16)
                    mixed[one, pl.ds(down, 16), across] = (real * cosine - imag * sine).astype(BF16)
                    mixed[one, pl.ds(rows + down, 16), across] = (real * sine + imag * cosine).astype(BF16)

    loop(firsts, one_first)


def core_dot(left, core_ref, sign, tile):
    half, part = left.shape[0] // 2, core_ref.shape[0]
    by_real = dot(left, core_ref[:, tile : tile + 256])
    by_imag = dot(left, core_ref[:, part + tile : part + tile + 256])
    if sign > 0:
        return by_real[:half] - by_imag[half:], by_real[half:] + by_imag[:half]
    return by_real[:half] + by_imag[half:], by_real[half:] - by_imag[:half]


def row_body(order, in_ref, mask_ref, core_ref, turn_ref, out_ref, mixed, passed, back):
    blocks, firsts, _, seconds, lanes = in_ref.shape
    radix, _, part = mixed.shape
    tiles = part // lanes
    rows = firsts * seconds
    row_mix(order, in_ref, turn_ref, mixed)

    def one(at):
        for tile in range(0, part, 256):
            real, imag = core_dot(mixed[at], core_ref, 1, tile)
            for within in range(0, 256, lanes):
                number = (tile + within) // lanes
                kept = mask_ref[number, at].astype(F32)
                across = pl.ds(tile + within, lanes)
                passed[pl.ds(0, rows), across] = (real[:, within : within + lanes] * kept).astype(BF16)
                passed[pl.ds(rows, rows), across] = (imag[:, within : within + lanes] * kept).astype(BF16)
        for tile in range(0, part, 256):
            real, imag = core_dot(passed[...], core_ref, -1, tile)
            across = pl.ds(tile, 256)
            cosine, sine = turn_ref[at, 0, :, across], turn_ref[at, 1, :, across]
            back[at, 0, :, across] = real * cosine + imag * sine
            back[at, 1, :, across] = imag * cosine - real * sine

    loop(radix, one)

    def close(first):
        for tile in range(tiles):
            across = pl.ds(tile * lanes, lanes)
            for at in range(0, seconds, 16):
                down = pl.ds(pl.multiple_of(first * seconds + at, 16), 16)
                values = [(back[one, 0, down, across], back[one, 1, down, across]) for one in range(radix)]
                for one, (real, imag) in enumerate(butterfly(values, -1)):
                    out_ref[order[one * tiles + tile], first, 0, pl.ds(at, 16)] = real.astype(BF16)
                    out_ref[order[one * tiles + tile], first, 1, pl.ds(at, 16)] = imag.astype(BF16)

    loop(firsts, close)


def row_work(order, received, mask, tables):
    blocks, firsts, _, seconds, lanes = received.shape
    core, turns = tables
    radix, part = turns.shape[0], core.shape[0]
    rows = firsts * seconds

    def body(*refs):
        row_body(order, *refs)

    return pl.pallas_call(
        body,
        out_shape=jax.ShapeDtypeStruct(received.shape, BF16),
        in_specs=vmem(4),
        out_specs=vmem(1)[0],
        scratch_shapes=[
            pltpu.VMEM((radix, 2 * rows, part), BF16),
            pltpu.VMEM((2 * rows, part), BF16),
            pltpu.VMEM((radix, 2, rows, part), F32),
        ],
        compiler_params=params(),
        name="row_both",
    )(received, mask, core, turns)


def last_row_body(order, in_ref, core_ref, turn_ref, out_ref, mixed):
    blocks, firsts, _, seconds, lanes = in_ref.shape
    radix, _, part = mixed.shape
    row_mix(order, in_ref, turn_ref, mixed)

    def one(at):
        for tile in range(0, part, 256):
            real, imag = core_dot(mixed[at], core_ref, 1, tile)
            for within in range(0, 256, lanes):
                number = (tile + within) // lanes
                out_ref[number, 0, at] = real[:, within : within + lanes].astype(BF16)
                out_ref[number, 1, at] = imag[:, within : within + lanes].astype(BF16)

    loop(radix, one)


def last_row_work(order, received, tables):
    blocks, firsts, _, seconds, lanes = received.shape
    core, turns = tables
    radix, part = turns.shape[0], core.shape[0]
    rows = firsts * seconds

    def body(*refs):
        last_row_body(order, *refs)

    return pl.pallas_call(
        body,
        out_shape=jax.ShapeDtypeStruct((part // lanes, 2, radix, rows, lanes), BF16),
        in_specs=vmem(3),
        out_specs=vmem(1)[0],
        scratch_shapes=[pltpu.VMEM((radix, 2 * rows, part), BF16)],
        compiler_params=params(),
        name="row_last",
    )(received, core, turns)


def mask_body(in_ref, down_ref, across_ref, out_ref):
    groups, radix, rows, lanes = out_ref.shape
    turned = dot(down_ref[...], in_ref[...].astype(BF16)).astype(BF16)
    for tile in range(0, radix * lanes, 256):
        got = dot(turned, across_ref[:, tile : tile + 256]).astype(BF16)
        for within in range(0, 256, lanes):
            out_ref[:, (tile + within) // lanes] = got[:, within : within + lanes].reshape(groups, rows, lanes)


def mask_work(transmission, row_count, col_count, radix):
    height, width = transmission.shape
    down = regroup(height, RADIX).T
    across = regroup(width, radix)
    return pl.pallas_call(
        mask_body,
        out_shape=jax.ShapeDtypeStruct((col_count, radix, height // col_count, width // radix), BF16),
        in_specs=vmem(3),
        out_specs=vmem(1)[0],
        compiler_params=params(),
        name="mask_order",
    )(transmission, jnp.asarray(down), jnp.asarray(across))


def closing_body(in_ref, keep_ref, down_ref, across_ref, out_ref, turned):
    groups, _, radix, rows, lanes = in_ref.shape
    for number in range(2):
        for at in range(radix):
            got = dot(down_ref[...], in_ref[:, number, at].reshape(groups * rows, lanes))
            turned[:, pl.ds(at * lanes, lanes)] = got.astype(BF16)
        for tile in range(0, radix * lanes, 256):
            across = pl.ds(tile, 256)
            out_ref[number, :, across] = dot(turned[...], across_ref[:, across]) * keep_ref[:, across]


def closing_work(received, transmission):
    groups, _, radix, rows, lanes = received.shape
    height, width = transmission.shape
    down = regroup(height, RADIX)
    across = regroup(width, radix).T
    return pl.pallas_call(
        closing_body,
        out_shape=jax.ShapeDtypeStruct((2, height, width), F32),
        in_specs=vmem(4),
        out_specs=vmem(1)[0],
        scratch_shapes=[pltpu.VMEM((height, width), BF16)],
        compiler_params=params(),
        name="closing_order",
    )(received, transmission, jnp.asarray(down), jnp.asarray(across))


def exchange(value, axis):
    return lax.all_to_all(value, axis, split_axis=0, concat_axis=0, tiled=True)


def widen(value):
    short = -value.shape[-1] % LANES
    return jnp.pad(value, [(0, 0)] * (value.ndim - 1) + [(0, short)]) if short else value


def on_device(spectrum, diffraction, order_mask, phases, transmission, shifts):
    height, wide = spectrum.shape[1:]
    row_count, col_count = lax.axis_size("rows"), lax.axis_size("cols")
    devices = row_count * col_count
    full_rows, full_cols = height * row_count, wide * col_count
    width = wide // row_count
    part = LANES * col_count
    radix = full_cols // part
    forward, backward = column_tables(full_rows)
    column_all = (jnp.asarray(forward), jnp.asarray(backward))
    core, turns = row_tables(full_cols, part)
    row_all = (jnp.asarray(core), jnp.asarray(turns))

    current = exchange(spectrum.reshape(2, height, row_count, width).transpose(2, 0, 1, 3), "rows")
    mats = lax.all_gather(diffraction, "rows", axis=0)
    mask_all = lax.all_gather(order_mask, "rows", axis=0).reshape(-1)
    angles = phases.astype(jnp.float16).reshape(BOUNCES, height, row_count, width).transpose(2, 0, 1, 3)
    angles = exchange(angles, "rows").astype(F32).transpose(1, 0, 2, 3).reshape(BOUNCES, full_rows, width)
    kept = exchange(mask_work(transmission, row_count, col_count, radix), "cols")

    narrow = width < LANES
    tiles = full_cols // LANES
    if narrow:
        order = list(range(tiles))
    else:
        order = [(at % row_count) * col_count + at // row_count for at in range(tiles)]

    def to_rows(value):
        got = exchange(value[..., :width].reshape(devices, *value.shape[2:-1], width), ("rows", "cols"))
        if not narrow:
            return got
        joined = LANES // width
        got = got.reshape(row_count, col_count, *got.shape[1:]).swapaxes(0, 1).reshape(tiles, joined, *got.shape[1:])
        return jnp.moveaxis(got, 1, -2).reshape(tiles, *got.shape[2:-1], LANES)

    def to_columns(value):
        if narrow:
            joined = LANES // width
            value = jnp.moveaxis(value.reshape(*value.shape[:-1], joined, width), -2, 1)
            value = value.reshape(col_count, row_count, *value.shape[2:]).swapaxes(0, 1)
            value = value.reshape(devices, *value.shape[2:])
        got = exchange(value, ("rows", "cols"))
        return widen(got.reshape(row_count, col_count, *got.shape[1:]))

    current = widen(current)
    for bounce in range(BOUNCES):
        sent = column_work(
            bounce > 0,
            current,
            mats,
            mask_all,
            shifts[bounce : bounce + 1],
            widen(angles[bounce]),
            column_all,
            row_count,
            col_count,
        )
        received = to_rows(sent)
        if bounce < BOUNCES - 1:
            current = to_columns(row_work(order, received, kept, row_all))
    worked = exchange(last_row_work(order, received, row_all), "cols")
    return closing_work(worked, transmission)


def solution(mesh):
    placed = (
        P(None, "rows", "cols"),
        P(None, "rows", None, None, None),
        P("rows", None),
        P(None, "rows", "cols"),
        P("rows", "cols"),
        P(),
    )
    return jax.shard_map(
        on_device, mesh=mesh, in_specs=placed, out_specs=P(None, "rows", "cols"), check_vma=False
    )
```

```python
import math

import jax
import jax.numpy as jnp
import ml_dtypes
import numpy as np
from jax import lax
from jax.experimental import pallas as pl
from jax.experimental.pallas import tpu as pltpu
from jax.sharding import PartitionSpec as P

BLOCK = 128
LANES = 128
RADIX = 16
BOUNCES = 2
GROUP = 4
ANGLE_STEPS = 10430.0
VMEM_LIMIT = 56 * 1024 * 1024
BF16 = jnp.bfloat16
F32 = jnp.float32


def params():
    return pltpu.CompilerParams(vmem_limit_bytes=VMEM_LIMIT)


def vmem(count):
    return [pl.BlockSpec(memory_space=pltpu.VMEM) for _ in range(count)]


def column_tables(extent):
    part = extent // RADIX
    first = np.arange(RADIX)[:, None, None]
    second = np.arange(part)[None, :, None]
    inner = np.arange(part)[None, None, :]
    angle = ((first + RADIX * second) * inner % extent) * (2.0 * np.pi / extent)
    scale = 1.0 / math.sqrt(extent)
    real, imag = np.cos(angle) * scale, np.sin(angle) * scale
    forward = np.concatenate([real, imag], axis=1)
    backward = np.concatenate([real.transpose(0, 2, 1), imag.transpose(0, 2, 1)], axis=1)
    return forward.astype(ml_dtypes.bfloat16), backward.astype(ml_dtypes.bfloat16)


def row_tables(extent, part):
    radix = extent // part
    inner = np.arange(part)
    angle = (inner[:, None] * inner[None, :] % part) * (2.0 * np.pi / part)
    scale = 1.0 / math.sqrt(extent)
    core = np.stack([np.cos(angle) * scale, np.sin(angle) * scale], axis=1)
    core = core.reshape(part, 2, part // LANES, LANES).transpose(2, 0, 1, 3).reshape(part // LANES, part, 2 * LANES)
    turn = (np.arange(radix)[:, None] * inner[None, :]) * (2.0 * np.pi / extent)
    turns = np.stack([np.cos(turn), np.sin(turn)], axis=1)[:, :, None, :]
    return core.astype(ml_dtypes.bfloat16), turns.astype(np.float32)


def regroup(count, fast):
    natural = np.arange(count)
    grouped = (natural % fast) * (count // fast) + natural // fast
    matrix = np.zeros((count, count), np.float32)
    matrix[natural, grouped] = 1.0
    return matrix.astype(ml_dtypes.bfloat16)


def half_series():
    top = (np.pi / 2) ** 2
    squares = (np.polynomial.chebyshev.chebpts1(200) + 1) * (top / 2)
    angles = np.sqrt(squares)

    def fit(values):
        series = np.polynomial.chebyshev.Chebyshev.fit(squares, values, 4, domain=[0, top])
        return [float(c) for c in series.convert(kind=np.polynomial.Polynomial).coef]

    return fit(np.sin(angles) / angles), fit(np.cos(angles))


SINE_SERIES, COSINE_SERIES = half_series()


def cos_sin(angle):
    half = angle * 0.5
    square = half * half

    def series(coefs):
        total = square * coefs[-1] + coefs[-2]
        for coef in coefs[-3::-1]:
            total = total * square + coef
        return total

    twice_sine, cosine = angle * series(SINE_SERIES), series(COSINE_SERIES)
    return 1.0 - twice_sine * twice_sine * 0.5, twice_sine * cosine


def butterfly(values, sign):
    count = len(values)
    if count == 1:
        return values
    even, odd = butterfly(values[0::2], sign), butterfly(values[1::2], sign)
    low, high = [], []
    for at in range(count // 2):
        real, imag = odd[at]
        if at == 0:
            turned = real, imag
        elif 4 * at == count:
            turned = (-imag, real) if sign > 0 else (imag, -real)
        elif 8 * at == count:
            half = math.sqrt(0.5)
            turned = (
                ((real - imag) * half, (real + imag) * half)
                if sign > 0
                else ((real + imag) * half, (imag - real) * half)
            )
        elif 8 * at == 3 * count:
            half = math.sqrt(0.5)
            turned = (
                ((real + imag) * -half, (real - imag) * half)
                if sign > 0
                else ((imag - real) * half, (real + imag) * -half)
            )
        else:
            cosine = math.cos(2 * math.pi * at / count)
            sine = sign * math.sin(2 * math.pi * at / count)
            turned = real * cosine - imag * sine, real * sine + imag * cosine
        low.append((even[at][0] + turned[0], even[at][1] + turned[1]))
        high.append((even[at][0] - turned[0], even[at][1] - turned[1]))
    return low + high


def dot(left, right):
    return jnp.dot(left, right, preferred_element_type=F32)


def loop(count, body, unroll=1):
    def step(at, carry):
        body(at)
        return carry

    lax.fori_loop(0, count, step, 0, unroll=min(unroll, count))


def aligned(start, size):
    return pl.ds(pl.multiple_of(start, size), size)


def column_body(later, peers, *refs):
    place_ref, shift_ref = refs[:2]
    current, refs = (refs[2:3], refs[3:]) if later else (refs[2 : 2 + peers], refs[2 + peers :])
    mats, refs = refs[: 2 * peers], refs[2 * peers :]
    angles, refs = refs[:peers], refs[peers:]
    tables, refs = refs[: 1 + later], refs[1 + later :]
    out_ref, padded, wave, mixed, held_mats, held_angles = refs[:6]
    held_tables, sems = refs[6:-1], refs[-1]
    rows_at, cols_at, firsts, _, seconds, width = out_ref.shape
    extent = wave.shape[1]
    part = extent // RADIX
    height = extent // peers
    half_blocks = height // BLOCK // 2

    copies = []

    def fetch(source, target):
        copy = pltpu.make_async_copy(source, target, sems.at[len(copies)])
        copy.start()
        copies.append(copy)
        return copy

    table_copies = [fetch(tables[-1], held_tables[-1])] if later else []
    mat_copies, angle_copies = [], []
    for at in range(peers):
        mat_copies.append([fetch(mats[2 * at + one], held_mats.at[at, one]) for one in range(2)])
        angle_copies.append(fetch(angles[at], held_angles.at[at]))
    table_copies.append(fetch(tables[0], held_tables[0]))

    padded[:, pl.ds(0, height)] = jnp.zeros((2, height, width), F32)
    padded[:, pl.ds(height + extent, height)] = jnp.zeros((2, height, width), F32)

    if later:
        cur_ref = current[0]
        table_copies[0].wait()

        def unfold(at):
            group, first = at // firsts, at % firsts
            real = cur_ref[:, group, first, 0].reshape(part, width)
            imag = cur_ref[:, group, first, 1].reshape(part, width)
            got = dot(held_tables[-1][at], jnp.concatenate([real, imag], axis=1))
            rows = aligned(at * part, part)
            wave[0, rows] = got[:part, :width] + got[part:, width:]
            wave[1, rows] = got[:part, width:] - got[part:, :width]

        loop(RADIX, unfold, 8)

        def gather(at):
            values = [
                (wave[0, aligned(one * part + at * 8, 8)], wave[1, aligned(one * part + at * 8, 8)])
                for one in range(RADIX)
            ]
            for one, (real, imag) in enumerate(butterfly(values, -1)):
                rows = aligned(height + one * part + at * 8, 8)
                padded[0, rows] = real
                padded[1, rows] = imag

        loop(part // 8, gather, 2)
    else:
        for at in range(peers):
            rows = aligned(height + (place_ref[0] ^ at) * height, height)
            padded[0, rows] = current[at][0].astype(F32)
            padded[1, rows] = current[at][1].astype(F32)

    shift = shift_ref[0]
    for at in range(peers):
        start = (place_ref[0] ^ at) * height
        for one in range(2):
            mat_copies[at][one].wait()
        angle_copies[at].wait()

        def diffract(block, at=at, start=start):
            within = block * BLOCK
            rights = []
            for order in range(3):
                rows = pl.ds(height + start + within + (order - 1) * shift, BLOCK)
                rights.append(jnp.concatenate([padded[0, rows], padded[1, rows]], axis=1).astype(BF16))
            left = held_mats[at, block // half_blocks, block % half_blocks]
            got = dot(left, jnp.concatenate(rights, axis=0))
            real = got[:BLOCK, :width] - got[BLOCK:, width:]
            imag = got[:BLOCK, width:] + got[BLOCK:, :width]
            cosine, sine = cos_sin(held_angles[at, aligned(within, BLOCK)].astype(F32) * (1.0 / ANGLE_STEPS))
            rows = aligned(start + within, BLOCK)
            wave[0, rows] = real * cosine - imag * sine
            wave[1, rows] = real * sine + imag * cosine

        loop(2 * half_blocks, diffract, 4)

    def mix(at):
        parts = []
        for half in range(2):
            down = at * 16 + half * 8
            values = [
                (wave[0, aligned(one * part + down, 8)], wave[1, aligned(one * part + down, 8)])
                for one in range(RADIX)
            ]
            parts.append(butterfly(values, 1))
        for one in range(RADIX):
            real, imag = (jnp.concatenate([parts[0][one][c], parts[1][one][c]], axis=0) for c in range(2))
            mixed[one, aligned(at * 16, 16)] = jnp.concatenate([real, imag], axis=1).astype(BF16)

    loop(part // 16, mix)
    table_copies[-1].wait()

    def fold(at):
        group, first = at // firsts, at % firsts
        got = dot(held_tables[0][at], mixed[at])
        real = (got[:part, :width] - got[part:, width:]).astype(BF16)
        imag = (got[:part, width:] + got[part:, :width]).astype(BF16)
        out_ref[:, group, first, 0] = real.reshape(rows_at, seconds, width)
        out_ref[:, group, first, 1] = imag.reshape(rows_at, seconds, width)

    loop(RADIX, fold, 8)


def column_work(later, place, shift, current, mats, angles, tables, col_count):
    peers = len(angles)
    height, width = angles[0].shape
    extent = height * peers
    part = extent // RADIX

    def body(*refs):
        column_body(later, peers, *refs)

    currents = [current] if later else current
    tables = tables if later else tables[:1]
    mats = [one for pair in mats for one in pair]
    smem, anywhere = pl.BlockSpec(memory_space=pltpu.SMEM), pl.BlockSpec(memory_space=pl.ANY)
    return pl.pallas_call(
        body,
        out_shape=jax.ShapeDtypeStruct((peers, col_count, RADIX // col_count, 2, part // peers, width), BF16),
        in_specs=[smem, smem] + vmem(len(currents)) + [anywhere] * (len(mats) + peers + len(tables)),
        out_specs=vmem(1)[0],
        scratch_shapes=[
            pltpu.VMEM((2, extent + 2 * height, width), F32),
            pltpu.VMEM((2, extent, width), F32),
            pltpu.VMEM((RADIX, part, 2 * width), BF16),
            pltpu.VMEM((peers, 2, *mats[0].shape), BF16),
            pltpu.VMEM((peers, height, width), angles[0].dtype),
            *[pltpu.VMEM(table.shape, BF16) for table in tables],
            pltpu.SemaphoreType.DMA((len(mats) + peers + len(tables),)),
        ],
        compiler_params=params(),
        name="column_later" if later else "column_first",
    )(place, shift, *currents, *mats, *angles, *tables)


def row_mix(order, in_ref, turn_ref, mixed):
    blocks, firsts, _, seconds, lanes = in_ref.shape
    radix, _, _, part = mixed.shape
    tiles = part // lanes

    def one_first(first):
        for tile in range(tiles):
            across = pl.ds(tile * lanes, lanes)
            for at in range(0, seconds, 16):
                values = [
                    (
                        in_ref[order[one * tiles + tile], first, 0, pl.ds(at, 16)].astype(F32),
                        in_ref[order[one * tiles + tile], first, 1, pl.ds(at, 16)].astype(F32),
                    )
                    for one in range(radix)
                ]
                for one, (real, imag) in enumerate(butterfly(values, 1)):
                    cosine, sine = turn_ref[one, 0, :, across], turn_ref[one, 1, :, across]
                    down = pl.multiple_of(first * seconds + at, 16)
                    mixed[one, 0, pl.ds(down, 16), across] = (real * cosine - imag * sine).astype(BF16)
                    mixed[one, 1, pl.ds(down, 16), across] = (real * sine + imag * cosine).astype(BF16)

    loop(firsts, one_first, 4)


def core_dot(left, tile_ref, sign):
    count, _, rows, depth = left.shape
    lanes = tile_ref.shape[1] // 2
    got = dot(left.reshape(count * 2 * rows, depth), tile_ref).reshape(count, 2, rows, 2 * lanes)
    first, second = got[:, 0], got[:, 1]
    if sign > 0:
        return first[..., :lanes] - second[..., lanes:], second[..., :lanes] + first[..., lanes:]
    return first[..., :lanes] + second[..., lanes:], second[..., :lanes] - first[..., lanes:]


def row_body(order, in_ref, mask_ref, core_ref, turn_ref, out_ref, mixed, passed, back):
    blocks, firsts, _, seconds, lanes = in_ref.shape
    radix, _, _, part = mixed.shape
    tiles = part // lanes
    rows = firsts * seconds
    row_mix(order, in_ref, turn_ref, mixed)
    at_once = min(GROUP, radix)

    for group in range(0, radix, at_once):
        these = pl.ds(group, at_once)

        def forward(tile, these=these):
            real, imag = core_dot(mixed[these], core_ref[tile], 1)
            kept = mask_ref[tile, these].astype(F32)
            across = aligned(tile * lanes, lanes)
            passed[these, 0, :, across] = (real * kept).astype(BF16)
            passed[these, 1, :, across] = (imag * kept).astype(BF16)

        loop(tiles, forward, tiles)

        def backward(tile, these=these):
            real, imag = core_dot(passed[these], core_ref[tile], -1)
            across = aligned(tile * lanes, lanes)
            cosine, sine = turn_ref[these, 0, :, across], turn_ref[these, 1, :, across]
            back[these, 0, :, across] = real * cosine + imag * sine
            back[these, 1, :, across] = imag * cosine - real * sine

        loop(tiles, backward, tiles)

    def close(first):
        for tile in range(tiles):
            across = pl.ds(tile * lanes, lanes)
            for at in range(0, seconds, 16):
                down = aligned(first * seconds + at, 16)
                values = [(back[one, 0, down, across], back[one, 1, down, across]) for one in range(radix)]
                for one, (real, imag) in enumerate(butterfly(values, -1)):
                    out_ref[order[one * tiles + tile], first, 0, pl.ds(at, 16)] = real.astype(BF16)
                    out_ref[order[one * tiles + tile], first, 1, pl.ds(at, 16)] = imag.astype(BF16)

    loop(firsts, close, 2)


def row_work(order, received, mask, tables):
    blocks, firsts, _, seconds, lanes = received.shape
    core, turns = tables
    radix, part = turns.shape[0], core.shape[1]
    rows = firsts * seconds

    def body(*refs):
        row_body(order, *refs)

    return pl.pallas_call(
        body,
        out_shape=jax.ShapeDtypeStruct(received.shape, BF16),
        in_specs=vmem(4),
        out_specs=vmem(1)[0],
        scratch_shapes=[
            pltpu.VMEM((radix, 2, rows, part), BF16),
            pltpu.VMEM((radix, 2, rows, part), BF16),
            pltpu.VMEM((radix, 2, rows, part), F32),
        ],
        compiler_params=params(),
        name="row_both",
    )(received, mask, core, turns)


def last_row_body(order, place_ref, in_ref, core_ref, turn_ref, *refs):
    mixed = refs[-1]
    radix = mixed.shape[0]
    at_once = min(GROUP, radix)
    row_mix(order, in_ref, turn_ref, mixed)
    for group in range(0, radix, at_once):
        these = pl.ds(group, at_once)
        for distance, out_ref in enumerate(refs[:-1]):
            real, imag = core_dot(mixed[these], core_ref[place_ref[0] ^ distance], 1)
            out_ref[0, these] = real.astype(BF16)
            out_ref[1, these] = imag.astype(BF16)


def last_row_work(order, place, received, tables, number, chunks):
    blocks, firsts, _, seconds, lanes = received.shape
    core, turns = tables
    radix, part = turns.shape[0], core.shape[1]
    seconds //= chunks
    rows = firsts * seconds

    def body(*refs):
        last_row_body(order, *refs)

    def whole(array):
        return pl.BlockSpec(array.shape, lambda i: (0,) * array.ndim)

    given = pl.BlockSpec((blocks, firsts, 2, seconds, lanes), lambda i: (0, 0, 0, number, 0))
    sent = jax.ShapeDtypeStruct((2, radix, rows, lanes), BF16)
    return pl.pallas_call(
        body,
        grid=(1,),
        out_shape=[sent] * (part // lanes),
        in_specs=[pl.BlockSpec(memory_space=pltpu.SMEM), given, whole(core), whole(turns)],
        out_specs=[whole(sent)] * (part // lanes),
        scratch_shapes=[pltpu.VMEM((radix, 2, rows, part), BF16)],
        compiler_params=params(),
        cost_estimate=pl.CostEstimate(flops=8 * rows * part * part * radix, bytes_accessed=2**22, transcendentals=0),
        name="row_last",
    )(place, received, core, turns)


def mask_body(in_ref, down_ref, across_ref, out_ref):
    groups, radix, rows, lanes = out_ref.shape
    turned = dot(down_ref[...], in_ref[...].astype(BF16)).astype(BF16)
    for tile in range(0, radix * lanes, 256):
        got = dot(turned, across_ref[:, tile : tile + 256]).astype(BF16)
        for within in range(0, 256, lanes):
            out_ref[:, (tile + within) // lanes] = got[:, within : within + lanes].reshape(groups, rows, lanes)


def mask_work(transmission, row_count, col_count, radix):
    height, width = transmission.shape
    down = regroup(height, RADIX).T
    across = regroup(width, radix)
    return pl.pallas_call(
        mask_body,
        out_shape=jax.ShapeDtypeStruct((col_count, radix, height // col_count, width // radix), BF16),
        in_specs=vmem(3),
        out_specs=vmem(1)[0],
        compiler_params=params(),
        name="mask_order",
    )(transmission, jnp.asarray(down), jnp.asarray(across))


def closing_body(groups, place_ref, *refs):
    given, (keep_ref, down_ref, across_ref), (out_ref, joined, turned) = refs[:groups], refs[groups : groups + 3], refs[-3:]
    _, radix, rows, lanes = given[0].shape
    for distance in range(groups):
        down = aligned((place_ref[0] ^ distance) * rows, rows)
        for number in range(2):
            for at in range(radix):
                joined[number, down, pl.ds(at * lanes, lanes)] = given[distance][number, at]
    for number in range(2):
        turned[number] = dot(down_ref[...], joined[number]).astype(BF16)
        for tile in range(0, radix * lanes, 256):
            across = pl.ds(tile, 256)
            out_ref[number, :, across] = dot(turned[number], across_ref[:, across]) * keep_ref[:, across]


def closing_work(place, received, transmission, earlier, number, chunks):
    groups = len(received)
    _, radix, rows, lanes = received[0].shape
    height, width = transmission.shape
    height //= chunks
    down = jnp.asarray(regroup(height, RADIX))
    across = jnp.asarray(regroup(width, radix).T)

    def body(*refs):
        closing_body(groups, *refs[: groups + 4], *refs[-3:])

    def whole(array):
        return pl.BlockSpec(array.shape, lambda i: (0,) * array.ndim)

    in_specs = [pl.BlockSpec(memory_space=pltpu.SMEM)] + [whole(one) for one in received]
    in_specs += [pl.BlockSpec((height, width), lambda i: (number, 0)), whole(down), whole(across)]
    arguments = [place, *received, transmission, down, across]
    aliases = {}
    if earlier is not None:
        aliases = {len(arguments): 0}
        in_specs.append(pl.BlockSpec(memory_space=pl.ANY))
        arguments.append(earlier)
    return pl.pallas_call(
        body,
        grid=(1,),
        out_shape=jax.ShapeDtypeStruct((2, height * chunks, width), F32),
        in_specs=in_specs,
        out_specs=pl.BlockSpec((2, height, width), lambda i: (0, number, 0)),
        scratch_shapes=[pltpu.VMEM((2, height, width), BF16), pltpu.VMEM((2, height, width), BF16)],
        input_output_aliases=aliases,
        compiler_params=params(),
        cost_estimate=pl.CostEstimate(flops=4 * height * width * width, bytes_accessed=2**22, transcendentals=0),
        name="closing_order",
    )(*arguments)


def exchange(value, axis):
    return lax.all_to_all(value, axis, split_axis=0, concat_axis=0, tiled=True)


def swap(value, axis, distance):
    if distance == 0:
        return value
    return lax.ppermute(value, axis, [(at, at ^ distance) for at in range(lax.axis_size(axis))])


def widen(value):
    short = -value.shape[-1] % LANES
    return jnp.pad(value, [(0, 0)] * (value.ndim - 1) + [(0, short)]) if short else value


def after(value, earlier):
    return lax.optimization_barrier((value, earlier))[0]


def gather_mats(mats):
    peers = lax.axis_size("rows")
    halves = mats[: mats.shape[0] // 2], mats[mats.shape[0] // 2 :]
    if peers != 8:
        result = [[swap(half, "rows", distance) for half in halves] for distance in range(peers)]
        return result, result[1]
    by_x = [swap(half, "rows", 2) for half in halves]
    by_y = [swap(half, "rows", 4) for half in halves]
    across = [swap(by_x[0], "rows", 4), swap(by_y[1], "rows", 2)]
    result = []
    for pair in (halves, by_x, by_y, across):
        result += [list(pair), [swap(half, "rows", 1) for half in pair]]
    return result, (by_x[0], by_y[1])


def on_device(spectrum, diffraction, order_mask, phases, transmission, shifts):
    height, wide = spectrum.shape[1:]
    row_count, col_count = lax.axis_size("rows"), lax.axis_size("cols")
    devices = row_count * col_count
    full_rows, full_cols = height * row_count, wide * col_count
    width = wide // row_count
    part = LANES * col_count
    radix = full_cols // part
    forward, backward = column_tables(full_rows)
    column_all = (jnp.asarray(forward), jnp.asarray(backward))
    core, turns = row_tables(full_cols, part)
    row_all = (jnp.asarray(core), jnp.asarray(turns))

    along, above = lax.axis_index("rows"), lax.axis_index("cols")
    place_rows, place_cols = (at.astype(jnp.int32).reshape(1) for at in (along, above))

    def spread(value):
        return [
            widen(swap(lax.dynamic_slice_in_dim(value, (along ^ distance) * width, width, value.ndim - 1), "rows", distance))
            for distance in range(row_count)
        ]

    masked = diffraction * order_mask.astype(BF16)[None, :, :, None, None]
    blocks = height // BLOCK
    masked = masked.transpose(1, 0, 3, 2, 4).reshape(blocks, 2 * BLOCK, 3 * BLOCK)
    mats, first_mats = gather_mats(masked)
    current = spread(after(spectrum, masked))
    codes = jnp.round(phases * ANGLE_STEPS).astype(jnp.int16)
    angles = [spread(after(codes[0], first_mats)), spread(codes[1])]
    kept = exchange(mask_work(transmission, row_count, col_count, radix), "cols")

    narrow = width < LANES
    tiles = full_cols // LANES
    if narrow:
        order = list(range(tiles))
    else:
        order = [(at % row_count) * col_count + at // row_count for at in range(tiles)]

    def to_rows(value):
        got = exchange(value[..., :width].reshape(devices, *value.shape[2:-1], width), ("rows", "cols"))
        if not narrow:
            return got
        joined = LANES // width
        got = got.reshape(row_count, col_count, *got.shape[1:]).swapaxes(0, 1).reshape(tiles, joined, *got.shape[1:])
        return jnp.moveaxis(got, 1, -2).reshape(tiles, *got.shape[2:-1], LANES)

    def to_columns(value):
        if narrow:
            joined = LANES // width
            value = jnp.moveaxis(value.reshape(*value.shape[:-1], joined, width), -2, 1)
            value = value.reshape(col_count, row_count, *value.shape[2:]).swapaxes(0, 1)
            value = value.reshape(devices, *value.shape[2:])
        got = exchange(value, ("rows", "cols"))
        return widen(got.reshape(row_count, col_count, *got.shape[1:]))

    for bounce in range(BOUNCES):
        sent = column_work(
            bounce > 0, place_rows, shifts[bounce : bounce + 1], current, mats, angles[bounce], column_all, col_count
        )
        received = to_rows(sent)
        if bounce < BOUNCES - 1:
            current = to_columns(row_work(order, received, kept, row_all))
    chunks = 2 if received.shape[3] % 32 == 0 else 1
    worked = [last_row_work(order, place_cols, received, row_all, number, chunks) for number in range(chunks)]
    worked = [[swap(one, "cols", distance) for distance, one in enumerate(chunk)] for chunk in worked]
    outgoing = None
    for number in range(chunks):
        outgoing = closing_work(place_cols, worked[number], transmission, outgoing, number, chunks)
    return outgoing


def solution(mesh):
    placed = (
        P(None, "rows", "cols"),
        P(None, "rows", None, None, None),
        P("rows", None),
        P(None, "rows", "cols"),
        P("rows", "cols"),
        P(),
    )
    return jax.shard_map(
        on_device, mesh=mesh, in_specs=placed, out_specs=P(None, "rows", "cols"), check_vma=False
    )
```

```python
import math

import jax
import jax.numpy as jnp
import ml_dtypes
import numpy as np
from jax import lax
from jax.experimental import pallas as pl
from jax.experimental.pallas import tpu as pltpu
from jax.sharding import PartitionSpec as P

BLOCK = 128
LANES = 128
RADIX = 16
BOUNCES = 2
GROUP = 4
ANGLE_STEPS = 10430.0
VMEM_LIMIT = 56 * 1024 * 1024
BF16 = jnp.bfloat16
F32 = jnp.float32


def params():
    return pltpu.CompilerParams(vmem_limit_bytes=VMEM_LIMIT)


def vmem(count):
    return [pl.BlockSpec(memory_space=pltpu.VMEM) for _ in range(count)]


def column_tables(extent):
    part = extent // RADIX
    first = np.arange(RADIX)[:, None, None]
    second = np.arange(part)[None, :, None]
    inner = np.arange(part)[None, None, :]
    angle = ((first + RADIX * second) * inner % extent) * (2.0 * np.pi / extent)
    scale = 1.0 / math.sqrt(extent)
    real, imag = np.cos(angle) * scale, np.sin(angle) * scale
    forward = np.concatenate([real, imag], axis=1)
    backward = np.concatenate([real.transpose(0, 2, 1), imag.transpose(0, 2, 1)], axis=1)
    return forward.astype(ml_dtypes.bfloat16), backward.astype(ml_dtypes.bfloat16)


def row_tables(extent, part):
    radix = extent // part
    inner = np.arange(part)
    angle = (inner[:, None] * inner[None, :] % part) * (2.0 * np.pi / part)
    scale = 1.0 / math.sqrt(extent)
    core = np.stack([np.cos(angle) * scale, np.sin(angle) * scale], axis=1)
    core = core.reshape(part, 2, part // LANES, LANES).transpose(2, 0, 1, 3).reshape(part // LANES, part, 2 * LANES)
    turn = (np.arange(radix)[:, None] * inner[None, :]) * (2.0 * np.pi / extent)
    turns = np.stack([np.cos(turn), np.sin(turn)], axis=1)[:, :, None, :]
    return core.astype(ml_dtypes.bfloat16), turns.astype(np.float32)


def regroup(count, fast):
    natural = np.arange(count)
    grouped = (natural % fast) * (count // fast) + natural // fast
    matrix = np.zeros((count, count), np.float32)
    matrix[natural, grouped] = 1.0
    return matrix.astype(ml_dtypes.bfloat16)


def half_series():
    top = (np.pi / 2) ** 2
    squares = (np.polynomial.chebyshev.chebpts1(200) + 1) * (top / 2)
    angles = np.sqrt(squares)

    def fit(values):
        series = np.polynomial.chebyshev.Chebyshev.fit(squares, values, 4, domain=[0, top])
        return [float(c) for c in series.convert(kind=np.polynomial.Polynomial).coef]

    return fit(np.sin(angles) / angles), fit(np.cos(angles))


SINE_SERIES, COSINE_SERIES = half_series()


def cos_sin(angle):
    half = angle * 0.5
    square = half * half

    def series(coefs):
        total = square * coefs[-1] + coefs[-2]
        for coef in coefs[-3::-1]:
            total = total * square + coef
        return total

    twice_sine, cosine = angle * series(SINE_SERIES), series(COSINE_SERIES)
    return 1.0 - twice_sine * twice_sine * 0.5, twice_sine * cosine


def butterfly(values, sign):
    count = len(values)
    if count == 1:
        return values
    even, odd = butterfly(values[0::2], sign), butterfly(values[1::2], sign)
    low, high = [], []
    for at in range(count // 2):
        real, imag = odd[at]
        if at == 0:
            turned = real, imag
        elif 4 * at == count:
            turned = (-imag, real) if sign > 0 else (imag, -real)
        elif 8 * at == count:
            half = math.sqrt(0.5)
            turned = (
                ((real - imag) * half, (real + imag) * half)
                if sign > 0
                else ((real + imag) * half, (imag - real) * half)
            )
        elif 8 * at == 3 * count:
            half = math.sqrt(0.5)
            turned = (
                ((real + imag) * -half, (real - imag) * half)
                if sign > 0
                else ((imag - real) * half, (real + imag) * -half)
            )
        else:
            cosine = math.cos(2 * math.pi * at / count)
            sine = sign * math.sin(2 * math.pi * at / count)
            turned = real * cosine - imag * sine, real * sine + imag * cosine
        low.append((even[at][0] + turned[0], even[at][1] + turned[1]))
        high.append((even[at][0] - turned[0], even[at][1] - turned[1]))
    return low + high


def dot(left, right):
    return jnp.dot(left, right, preferred_element_type=F32)


def loop(count, body, unroll=1):
    def step(at, carry):
        body(at)
        return carry

    lax.fori_loop(0, count, step, 0, unroll=min(unroll, count))


def aligned(start, size):
    return pl.ds(pl.multiple_of(start, size), size)


def by_distance(pieces, distance):
    return pieces[-1].at[distance // 2] if distance % 2 else pieces[distance // 2]


def column_body(later, peers, counts, *refs):
    (place_ref, shift_ref), refs = refs[:2], refs[2:]
    groups = []
    for count in counts:
        groups.append(refs[:count])
        refs = refs[count:]
    current, *mats, angles, tables = groups
    out_ref, padded, wave, mixed, held_mats, held_angles = refs[:6]
    held_tables, sems = refs[6:-1], refs[-1]
    rows_at, cols_at, firsts, _, seconds, width = out_ref.shape
    extent = wave.shape[1]
    part = extent // RADIX
    height = extent // peers
    own_blocks = height // BLOCK

    copies = []

    def fetch(source, target):
        copy = pltpu.make_async_copy(source, target, sems.at[len(copies)])
        copy.start()
        copies.append(copy)
        return copy

    table_copies = [fetch(tables[-1], held_tables[-1])] if later else []
    mat_copies, angle_copies = [], []
    for at in range(peers):
        first, some = 0, []
        for piece in mats[at]:
            some.append(fetch(piece, held_mats.at[at, pl.ds(first, piece.shape[0])]))
            first += piece.shape[0]
        mat_copies.append(some)
        angle_copies.append(fetch(by_distance(angles, at), held_angles.at[at]))
    table_copies.append(fetch(tables[0], held_tables[0]))

    padded[:, pl.ds(0, height)] = jnp.zeros((2, height, width), F32)
    padded[:, pl.ds(height + extent, height)] = jnp.zeros((2, height, width), F32)

    if later:
        cur_ref = current[0]
        table_copies[0].wait()

        def unfold(at):
            group, first = at // firsts, at % firsts
            real = cur_ref[:, group, first, 0].reshape(part, width)
            imag = cur_ref[:, group, first, 1].reshape(part, width)
            got = dot(held_tables[-1][at], jnp.concatenate([real, imag], axis=1))
            rows = aligned(at * part, part)
            wave[0, rows] = got[:part, :width] + got[part:, width:]
            wave[1, rows] = got[:part, width:] - got[part:, :width]

        loop(RADIX, unfold, 8)

        def gather(at):
            values = [
                (wave[0, aligned(one * part + at * 8, 8)], wave[1, aligned(one * part + at * 8, 8)])
                for one in range(RADIX)
            ]
            for one, (real, imag) in enumerate(butterfly(values, -1)):
                rows = aligned(height + one * part + at * 8, 8)
                padded[0, rows] = real
                padded[1, rows] = imag

        loop(part // 8, gather, 2)
    else:
        for at in range(peers):
            rows = aligned(height + (place_ref[0] ^ at) * height, height)
            piece = by_distance(current, at)
            padded[0, rows] = piece[0].astype(F32)
            padded[1, rows] = piece[1].astype(F32)

    shift = shift_ref[0]
    for at in range(peers):
        start = (place_ref[0] ^ at) * height
        for copy in mat_copies[at]:
            copy.wait()
        angle_copies[at].wait()

        def diffract(block, at=at, start=start):
            within = block * BLOCK
            rights = []
            for order in range(3):
                rows = pl.ds(height + start + within + (order - 1) * shift, BLOCK)
                rights.append(jnp.concatenate([padded[0, rows], padded[1, rows]], axis=1).astype(BF16))
            got = dot(held_mats[at, block], jnp.concatenate(rights, axis=0))
            real = got[:BLOCK, :width] - got[BLOCK:, width:]
            imag = got[:BLOCK, width:] + got[BLOCK:, :width]
            cosine, sine = cos_sin(held_angles[at, aligned(within, BLOCK)].astype(F32) * (1.0 / ANGLE_STEPS))
            rows = aligned(start + within, BLOCK)
            wave[0, rows] = real * cosine - imag * sine
            wave[1, rows] = real * sine + imag * cosine

        loop(own_blocks, diffract, 4)

    def mix(at):
        parts = []
        for half in range(2):
            down = at * 16 + half * 8
            values = [
                (wave[0, aligned(one * part + down, 8)], wave[1, aligned(one * part + down, 8)])
                for one in range(RADIX)
            ]
            parts.append(butterfly(values, 1))
        for one in range(RADIX):
            real, imag = (jnp.concatenate([parts[0][one][c], parts[1][one][c]], axis=0) for c in range(2))
            mixed[one, aligned(at * 16, 16)] = jnp.concatenate([real, imag], axis=1).astype(BF16)

    loop(part // 16, mix)
    table_copies[-1].wait()

    def fold(at):
        group, first = at // firsts, at % firsts
        got = dot(held_tables[0][at], mixed[at])
        real = (got[:part, :width] - got[part:, width:]).astype(BF16)
        imag = (got[:part, width:] + got[part:, :width]).astype(BF16)
        out_ref[:, group, first, 0] = real.reshape(rows_at, seconds, width)
        out_ref[:, group, first, 1] = imag.reshape(rows_at, seconds, width)

    loop(RADIX, fold, 8)


def column_work(later, place, shift, current, mats, angles, tables, col_count):
    peers = len(mats)
    height, width = angles[0].shape
    extent = height * peers
    part = extent // RADIX
    groups = [[current] if later else current, *mats, angles, tables if later else tables[:1]]
    counts = [len(group) for group in groups]
    copies = sum(counts[1:-2]) + peers + counts[-1]

    def body(*refs):
        column_body(later, peers, counts, *refs)

    smem, anywhere = pl.BlockSpec(memory_space=pltpu.SMEM), pl.BlockSpec(memory_space=pl.ANY)
    return pl.pallas_call(
        body,
        out_shape=jax.ShapeDtypeStruct((peers, col_count, RADIX // col_count, 2, part // peers, width), BF16),
        in_specs=[smem, smem] + vmem(counts[0]) + [anywhere] * sum(counts[1:]),
        out_specs=vmem(1)[0],
        scratch_shapes=[
            pltpu.VMEM((2, extent + 2 * height, width), F32),
            pltpu.VMEM((2, extent, width), F32),
            pltpu.VMEM((RADIX, part, 2 * width), BF16),
            pltpu.VMEM((peers, height // BLOCK, 2 * BLOCK, 3 * BLOCK), BF16),
            pltpu.VMEM((peers, height, width), angles[0].dtype),
            *[pltpu.VMEM(table.shape, BF16) for table in groups[-1]],
            pltpu.SemaphoreType.DMA((copies,)),
        ],
        compiler_params=params(),
        name="column_later" if later else "column_first",
    )(place, shift, *[one for group in groups for one in group])


def row_mix(order, in_ref, turn_ref, mixed):
    blocks, firsts, _, seconds, lanes = in_ref.shape
    radix, _, _, part = mixed.shape
    tiles = part // lanes

    def one_first(first):
        for tile in range(tiles):
            across = pl.ds(tile * lanes, lanes)
            for at in range(0, seconds, 16):
                values = [
                    (
                        in_ref[order[one * tiles + tile], first, 0, pl.ds(at, 16)].astype(F32),
                        in_ref[order[one * tiles + tile], first, 1, pl.ds(at, 16)].astype(F32),
                    )
                    for one in range(radix)
                ]
                for one, (real, imag) in enumerate(butterfly(values, 1)):
                    cosine, sine = turn_ref[one, 0, :, across], turn_ref[one, 1, :, across]
                    down = pl.multiple_of(first * seconds + at, 16)
                    mixed[one, 0, pl.ds(down, 16), across] = (real * cosine - imag * sine).astype(BF16)
                    mixed[one, 1, pl.ds(down, 16), across] = (real * sine + imag * cosine).astype(BF16)

    loop(firsts, one_first, 4)


def core_dot(left, tile_ref, sign):
    count, _, rows, depth = left.shape
    lanes = tile_ref.shape[1] // 2
    got = dot(left.reshape(count * 2 * rows, depth), tile_ref).reshape(count, 2, rows, 2 * lanes)
    first, second = got[:, 0], got[:, 1]
    if sign > 0:
        return first[..., :lanes] - second[..., lanes:], second[..., :lanes] + first[..., lanes:]
    return first[..., :lanes] + second[..., lanes:], second[..., :lanes] - first[..., lanes:]


def row_body(order, in_ref, mask_ref, core_ref, turn_ref, out_ref, mixed, passed, back):
    blocks, firsts, _, seconds, lanes = in_ref.shape
    radix, _, _, part = mixed.shape
    tiles = part // lanes
    rows = firsts * seconds
    row_mix(order, in_ref, turn_ref, mixed)
    at_once = min(GROUP, radix)

    for group in range(0, radix, at_once):
        these = pl.ds(group, at_once)

        def forward(tile, these=these):
            real, imag = core_dot(mixed[these], core_ref[tile], 1)
            kept = mask_ref[tile, these].astype(F32)
            across = aligned(tile * lanes, lanes)
            passed[these, 0, :, across] = (real * kept).astype(BF16)
            passed[these, 1, :, across] = (imag * kept).astype(BF16)

        loop(tiles, forward, tiles)

        def backward(tile, these=these):
            real, imag = core_dot(passed[these], core_ref[tile], -1)
            across = aligned(tile * lanes, lanes)
            cosine, sine = turn_ref[these, 0, :, across], turn_ref[these, 1, :, across]
            back[these, 0, :, across] = real * cosine + imag * sine
            back[these, 1, :, across] = imag * cosine - real * sine

        loop(tiles, backward, tiles)

    def close(first):
        for tile in range(tiles):
            across = pl.ds(tile * lanes, lanes)
            for at in range(0, seconds, 16):
                down = aligned(first * seconds + at, 16)
                values = [(back[one, 0, down, across], back[one, 1, down, across]) for one in range(radix)]
                for one, (real, imag) in enumerate(butterfly(values, -1)):
                    out_ref[order[one * tiles + tile], first, 0, pl.ds(at, 16)] = real.astype(BF16)
                    out_ref[order[one * tiles + tile], first, 1, pl.ds(at, 16)] = imag.astype(BF16)

    loop(firsts, close, 2)


def row_work(order, received, mask, tables):
    blocks, firsts, _, seconds, lanes = received.shape
    core, turns = tables
    radix, part = turns.shape[0], core.shape[1]
    rows = firsts * seconds

    def body(*refs):
        row_body(order, *refs)

    return pl.pallas_call(
        body,
        out_shape=jax.ShapeDtypeStruct(received.shape, BF16),
        in_specs=vmem(4),
        out_specs=vmem(1)[0],
        scratch_shapes=[
            pltpu.VMEM((radix, 2, rows, part), BF16),
            pltpu.VMEM((radix, 2, rows, part), BF16),
            pltpu.VMEM((radix, 2, rows, part), F32),
        ],
        compiler_params=params(),
        name="row_both",
    )(received, mask, core, turns)


def last_row_body(order, place_ref, in_ref, core_ref, turn_ref, *refs):
    mixed = refs[-1]
    radix = mixed.shape[0]
    at_once = min(GROUP, radix)
    row_mix(order, in_ref, turn_ref, mixed)
    for group in range(0, radix, at_once):
        these = pl.ds(group, at_once)
        for distance, out_ref in enumerate(refs[:-1]):
            real, imag = core_dot(mixed[these], core_ref[place_ref[0] ^ distance], 1)
            out_ref[0, these] = real.astype(BF16)
            out_ref[1, these] = imag.astype(BF16)


def last_row_work(order, place, received, tables, number, chunks):
    blocks, firsts, _, seconds, lanes = received.shape
    core, turns = tables
    radix, part = turns.shape[0], core.shape[1]
    seconds //= chunks
    rows = firsts * seconds

    def body(*refs):
        last_row_body(order, *refs)

    def whole(array):
        return pl.BlockSpec(array.shape, lambda i: (0,) * array.ndim)

    given = pl.BlockSpec((blocks, firsts, 2, seconds, lanes), lambda i: (0, 0, 0, number, 0))
    sent = jax.ShapeDtypeStruct((2, radix, rows, lanes), BF16)
    return pl.pallas_call(
        body,
        grid=(1,),
        out_shape=[sent] * (part // lanes),
        in_specs=[pl.BlockSpec(memory_space=pltpu.SMEM), given, whole(core), whole(turns)],
        out_specs=[whole(sent)] * (part // lanes),
        scratch_shapes=[pltpu.VMEM((radix, 2, rows, part), BF16)],
        compiler_params=params(),
        cost_estimate=pl.CostEstimate(flops=8 * rows * part * part * radix, bytes_accessed=2**22, transcendentals=0),
        name="row_last",
    )(place, received, core, turns)


def mask_body(in_ref, down_ref, across_ref, out_ref):
    groups, radix, rows, lanes = out_ref.shape
    turned = dot(down_ref[...], in_ref[...].astype(BF16)).astype(BF16)
    for tile in range(0, radix * lanes, 256):
        got = dot(turned, across_ref[:, tile : tile + 256]).astype(BF16)
        for within in range(0, 256, lanes):
            out_ref[:, (tile + within) // lanes] = got[:, within : within + lanes].reshape(groups, rows, lanes)


def mask_work(transmission, row_count, col_count, radix):
    height, width = transmission.shape
    down = regroup(height, RADIX).T
    across = regroup(width, radix)
    return pl.pallas_call(
        mask_body,
        out_shape=jax.ShapeDtypeStruct((col_count, radix, height // col_count, width // radix), BF16),
        in_specs=vmem(3),
        out_specs=vmem(1)[0],
        compiler_params=params(),
        name="mask_order",
    )(transmission, jnp.asarray(down), jnp.asarray(across))


def closing_body(groups, place_ref, *refs):
    given, (keep_ref, down_ref, across_ref), (out_ref, joined, turned) = refs[:groups], refs[groups : groups + 3], refs[-3:]
    _, radix, rows, lanes = given[0].shape
    for distance in range(groups):
        down = aligned((place_ref[0] ^ distance) * rows, rows)
        for number in range(2):
            for at in range(radix):
                joined[number, down, pl.ds(at * lanes, lanes)] = given[distance][number, at]
    for number in range(2):
        turned[number] = dot(down_ref[...], joined[number]).astype(BF16)
        for tile in range(0, radix * lanes, 256):
            across = pl.ds(tile, 256)
            out_ref[number, :, across] = dot(turned[number], across_ref[:, across]) * keep_ref[:, across]


def closing_work(place, received, transmission, earlier, number, chunks):
    groups = len(received)
    _, radix, rows, lanes = received[0].shape
    height, width = transmission.shape
    height //= chunks
    down = jnp.asarray(regroup(height, RADIX))
    across = jnp.asarray(regroup(width, radix).T)

    def body(*refs):
        closing_body(groups, *refs[: groups + 4], *refs[-3:])

    def whole(array):
        return pl.BlockSpec(array.shape, lambda i: (0,) * array.ndim)

    in_specs = [pl.BlockSpec(memory_space=pltpu.SMEM)] + [whole(one) for one in received]
    in_specs += [pl.BlockSpec((height, width), lambda i: (number, 0)), whole(down), whole(across)]
    arguments = [place, *received, transmission, down, across]
    aliases = {}
    if earlier is not None:
        aliases = {len(arguments): 0}
        in_specs.append(pl.BlockSpec(memory_space=pl.ANY))
        arguments.append(earlier)
    return pl.pallas_call(
        body,
        grid=(1,),
        out_shape=jax.ShapeDtypeStruct((2, height * chunks, width), F32),
        in_specs=in_specs,
        out_specs=pl.BlockSpec((2, height, width), lambda i: (0, number, 0)),
        scratch_shapes=[pltpu.VMEM((2, height, width), BF16), pltpu.VMEM((2, height, width), BF16)],
        input_output_aliases=aliases,
        compiler_params=params(),
        cost_estimate=pl.CostEstimate(flops=4 * height * width * width, bytes_accessed=2**22, transcendentals=0),
        name="closing_order",
    )(*arguments)


def exchange(value, axis):
    return lax.all_to_all(value, axis, split_axis=0, concat_axis=0, tiled=True)


def swap(value, axis, distance):
    if distance == 0:
        return value
    return lax.ppermute(value, axis, [(at, at ^ distance) for at in range(lax.axis_size(axis))])


def widen(value):
    short = -value.shape[-1] % LANES
    return jnp.pad(value, [(0, 0)] * (value.ndim - 1) + [(0, short)]) if short else value


def after(value, earlier):
    return lax.optimization_barrier((value, earlier))[0]


def gather_mats(mats):
    peers = lax.axis_size("rows")
    if peers != 8:
        result = [[swap(mats, "rows", distance)] for distance in range(peers)]
        return result, result[1]
    half = mats.shape[0] // 2
    by_x, by_y = swap(mats, "rows", 2), swap(mats, "rows", 4)
    across = [swap(by_x[:half], "rows", 4), swap(by_y[half:], "rows", 2)]
    result = []
    for pieces in ([mats], [by_x], [by_y], across):
        result += [pieces, [swap(piece, "rows", 1) for piece in pieces]]
    return result, (by_x, by_y)


def spread(value, width):
    peers, along = lax.axis_size("rows"), lax.axis_index("rows")
    chips = []
    for distance in range(0, peers, 2):
        start = ((along ^ distance) // 2) * (2 * width)
        piece = lax.dynamic_slice_in_dim(value, start, 2 * width, value.ndim - 1)
        chips.append(swap(piece, "rows", distance))

    def part(piece, core):
        return lax.dynamic_slice_in_dim(piece, core * width, width, value.ndim - 1)

    core = along % 2
    other = swap(jnp.stack([part(piece, 1 - core) for piece in chips]), "rows", 1)
    return [widen(part(piece, core)) for piece in chips] + [widen(other)]


def on_device(spectrum, diffraction, order_mask, phases, transmission, shifts):
    height, wide = spectrum.shape[1:]
    row_count, col_count = lax.axis_size("rows"), lax.axis_size("cols")
    devices = row_count * col_count
    full_rows, full_cols = height * row_count, wide * col_count
    width = wide // row_count
    part = LANES * col_count
    radix = full_cols // part
    forward, backward = column_tables(full_rows)
    column_all = (jnp.asarray(forward), jnp.asarray(backward))
    core, turns = row_tables(full_cols, part)
    row_all = (jnp.asarray(core), jnp.asarray(turns))

    along, above = lax.axis_index("rows"), lax.axis_index("cols")
    place_rows, place_cols = (at.astype(jnp.int32).reshape(1) for at in (along, above))

    masked = diffraction * order_mask.astype(BF16)[None, :, :, None, None]
    blocks = height // BLOCK
    masked = masked.transpose(1, 0, 3, 2, 4).reshape(blocks, 2 * BLOCK, 3 * BLOCK)
    mats, first_mats = gather_mats(masked)
    current = spread(spectrum, width)
    codes = jnp.round(phases * ANGLE_STEPS).astype(jnp.int16)
    angles = [spread(codes[0], width), spread(codes[1], width)]
    kept = exchange(mask_work(transmission, row_count, col_count, radix), "cols")

    narrow = width < LANES
    tiles = full_cols // LANES
    if narrow:
        order = list(range(tiles))
    else:
        order = [(at % row_count) * col_count + at // row_count for at in range(tiles)]

    def to_rows(value):
        got = exchange(value[..., :width].reshape(devices, *value.shape[2:-1], width), ("rows", "cols"))
        if not narrow:
            return got
        joined = LANES // width
        got = got.reshape(row_count, col_count, *got.shape[1:]).swapaxes(0, 1).reshape(tiles, joined, *got.shape[1:])
        return jnp.moveaxis(got, 1, -2).reshape(tiles, *got.shape[2:-1], LANES)

    def to_columns(value):
        if narrow:
            joined = LANES // width
            value = jnp.moveaxis(value.reshape(*value.shape[:-1], joined, width), -2, 1)
            value = value.reshape(col_count, row_count, *value.shape[2:]).swapaxes(0, 1)
            value = value.reshape(devices, *value.shape[2:])
        got = exchange(value, ("rows", "cols"))
        return widen(got.reshape(row_count, col_count, *got.shape[1:]))

    for bounce in range(BOUNCES):
        sent = column_work(
            bounce > 0, place_rows, shifts[bounce : bounce + 1], current, mats, angles[bounce], column_all, col_count
        )
        received = to_rows(sent)
        if bounce < BOUNCES - 1:
            current = to_columns(row_work(order, received, kept, row_all))
    chunks = 2 if received.shape[3] % 32 == 0 else 1
    worked = [last_row_work(order, place_cols, received, row_all, number, chunks) for number in range(chunks)]
    worked = [[swap(one, "cols", distance) for distance, one in enumerate(chunk)] for chunk in worked]
    outgoing = None
    for number in range(chunks):
        outgoing = closing_work(place_cols, worked[number], transmission, outgoing, number, chunks)
    return outgoing


def solution(mesh):
    placed = (
        P(None, "rows", "cols"),
        P(None, "rows", None, None, None),
        P("rows", None),
        P(None, "rows", "cols"),
        P("rows", "cols"),
        P(),
    )
    return jax.shard_map(
        on_device, mesh=mesh, in_specs=placed, out_specs=P(None, "rows", "cols"), check_vma=False
    )
```

```python
import math

import jax
import jax.numpy as jnp
import ml_dtypes
import numpy as np
from jax import lax
from jax.experimental import pallas as pl
from jax.experimental.pallas import tpu as pltpu
from jax.sharding import PartitionSpec as P

BLOCK = 128
LANES = 128
RADIX = 16
BOUNCES = 2
GROUP = 4
ANGLE_STEPS = 10430.0
VMEM_LIMIT = 62 * 1024 * 1024
BF16 = jnp.bfloat16
F32 = jnp.float32


def params():
    return pltpu.CompilerParams(vmem_limit_bytes=VMEM_LIMIT)


def vmem(count):
    return [pl.BlockSpec(memory_space=pltpu.VMEM) for _ in range(count)]


def column_tables(extent):
    part = extent // RADIX
    first = np.arange(RADIX)[:, None, None]
    second = np.arange(part)[None, :, None]
    inner = np.arange(part)[None, None, :]
    angle = ((first + RADIX * second) * inner % extent) * (2.0 * np.pi / extent)
    scale = 1.0 / math.sqrt(extent)
    real, imag = np.cos(angle) * scale, np.sin(angle) * scale
    forward = np.concatenate([real, imag], axis=1)
    backward = np.concatenate([real.transpose(0, 2, 1), imag.transpose(0, 2, 1)], axis=1)
    return forward.astype(ml_dtypes.bfloat16), backward.astype(ml_dtypes.bfloat16)


def row_tables(extent, part):
    radix = extent // part
    inner = np.arange(part)
    angle = (inner[:, None] * inner[None, :] % part) * (2.0 * np.pi / part)
    scale = 1.0 / math.sqrt(extent)
    core = np.stack([np.cos(angle) * scale, np.sin(angle) * scale], axis=1)
    core = core.reshape(part, 2, part // LANES, LANES).transpose(2, 0, 1, 3).reshape(part // LANES, part, 2 * LANES)
    turn = (np.arange(radix)[:, None] * inner[None, :]) * (2.0 * np.pi / extent)
    turns = np.stack([np.cos(turn), np.sin(turn)], axis=1)[:, :, None, :]
    return core.astype(ml_dtypes.bfloat16), turns.astype(np.float32)


def regroup(count, fast):
    natural = np.arange(count)
    grouped = (natural % fast) * (count // fast) + natural // fast
    matrix = np.zeros((count, count), np.float32)
    matrix[natural, grouped] = 1.0
    return matrix.astype(ml_dtypes.bfloat16)


def half_series():
    top = (np.pi / 2) ** 2
    squares = (np.polynomial.chebyshev.chebpts1(200) + 1) * (top / 2)
    angles = np.sqrt(squares)

    def fit(values):
        series = np.polynomial.chebyshev.Chebyshev.fit(squares, values, 4, domain=[0, top])
        return [float(c) for c in series.convert(kind=np.polynomial.Polynomial).coef]

    return fit(np.sin(angles) / angles), fit(np.cos(angles))


SINE_SERIES, COSINE_SERIES = half_series()


def cos_sin(angle):
    half = angle * 0.5
    square = half * half

    def series(coefs):
        total = square * coefs[-1] + coefs[-2]
        for coef in coefs[-3::-1]:
            total = total * square + coef
        return total

    twice_sine, cosine = angle * series(SINE_SERIES), series(COSINE_SERIES)
    return 1.0 - twice_sine * twice_sine * 0.5, twice_sine * cosine


def butterfly(values, sign):
    count = len(values)
    if count == 1:
        return values
    even, odd = butterfly(values[0::2], sign), butterfly(values[1::2], sign)
    low, high = [], []
    for at in range(count // 2):
        real, imag = odd[at]
        if at == 0:
            turned = real, imag
        elif 4 * at == count:
            turned = (-imag, real) if sign > 0 else (imag, -real)
        elif 8 * at == count:
            half = math.sqrt(0.5)
            turned = (
                ((real - imag) * half, (real + imag) * half)
                if sign > 0
                else ((real + imag) * half, (imag - real) * half)
            )
        elif 8 * at == 3 * count:
            half = math.sqrt(0.5)
            turned = (
                ((real + imag) * -half, (real - imag) * half)
                if sign > 0
                else ((imag - real) * half, (real + imag) * -half)
            )
        else:
            cosine = math.cos(2 * math.pi * at / count)
            sine = sign * math.sin(2 * math.pi * at / count)
            turned = real * cosine - imag * sine, real * sine + imag * cosine
        low.append((even[at][0] + turned[0], even[at][1] + turned[1]))
        high.append((even[at][0] - turned[0], even[at][1] - turned[1]))
    return low + high


def dot(left, right):
    return jnp.dot(left, right, preferred_element_type=F32)


def loop(count, body, unroll=1):
    def step(at, carry):
        body(at)
        return carry

    lax.fori_loop(0, count, step, 0, unroll=min(unroll, count))


def aligned(start, size):
    return pl.ds(pl.multiple_of(start, size), size)


def by_distance(pieces, distance):
    return pieces[-1].at[distance // 2] if distance % 2 else pieces[distance // 2]


def column_body(later, peers, counts, *refs):
    (place_ref, shift_ref), refs = refs[:2], refs[2:]
    groups = []
    for count in counts:
        groups.append(refs[:count])
        refs = refs[count:]
    current, *mats, angles, tables = groups
    out_ref, padded, wave, mixed, held_current, held_mats, held_angles, held_out = refs[:8]
    held_tables, sems = refs[8:-1], refs[-1]
    rows_at, cols_at, firsts, _, seconds, width = out_ref.shape
    extent = wave.shape[1]
    part = extent // RADIX
    height = extent // peers
    own_blocks = height // BLOCK

    copies = []

    def fetch(source, target):
        copy = pltpu.make_async_copy(source, target, sems.at[len(copies)])
        copy.start()
        copies.append(copy)
        return copy

    def fetch_table(number, group):
        mine = pl.ds(group * firsts, firsts)
        return fetch(tables[number].at[mine], held_tables[number].at[mine])

    if later:
        current_copies = []
        for group in range(cols_at):
            some = [fetch(current[0].at[:, group], held_current.at[:, group]), fetch_table(1, group)]
            current_copies.append(some)
    else:
        current_copies = [
            fetch(by_distance(current, at), held_current.at[at]) for at in range(peers)
        ]
    mat_copies, angle_copies = [], []
    for at in range(peers):
        first, some = 0, []
        for piece in mats[at]:
            some.append(fetch(piece, held_mats.at[at, pl.ds(first, piece.shape[0])]))
            first += piece.shape[0]
        mat_copies.append(some)
        angle_copies.append(fetch(by_distance(angles, at), held_angles.at[at]))
    table_copies = [fetch_table(0, group) for group in range(cols_at)]

    padded[:, pl.ds(0, height)] = jnp.zeros((2, height, width), F32)
    padded[:, pl.ds(height + extent, height)] = jnp.zeros((2, height, width), F32)

    if later:
        for group in range(cols_at):
            for copy in current_copies[group]:
                copy.wait()

            def unfold(first, group=group):
                at = group * firsts + first
                real = held_current[:, group, first, 0].reshape(part, width)
                imag = held_current[:, group, first, 1].reshape(part, width)
                got = dot(held_tables[-1][at], jnp.concatenate([real, imag], axis=1))
                rows = aligned(at * part, part)
                wave[0, rows] = got[:part, :width] + got[part:, width:]
                wave[1, rows] = got[:part, width:] - got[part:, :width]

            loop(firsts, unfold, firsts)

        def gather(at):
            values = [
                (wave[0, aligned(one * part + at * 8, 8)], wave[1, aligned(one * part + at * 8, 8)])
                for one in range(RADIX)
            ]
            for one, (real, imag) in enumerate(butterfly(values, -1)):
                rows = aligned(height + one * part + at * 8, 8)
                padded[0, rows] = real
                padded[1, rows] = imag

        loop(part // 8, gather, 2)
    else:
        for at in range(peers):
            rows = aligned(height + (place_ref[0] ^ at) * height, height)
            current_copies[at].wait()
            padded[0, rows] = held_current[at, 0].astype(F32)
            padded[1, rows] = held_current[at, 1].astype(F32)

    shift = shift_ref[0]
    for at in range(peers):
        start = (place_ref[0] ^ at) * height
        for copy in mat_copies[at]:
            copy.wait()
        angle_copies[at].wait()

        def diffract(block, at=at, start=start):
            within = block * BLOCK
            rights = []
            for order in range(3):
                rows = pl.ds(height + start + within + (order - 1) * shift, BLOCK)
                rights.append(jnp.concatenate([padded[0, rows], padded[1, rows]], axis=1).astype(BF16))
            got = dot(held_mats[at, block], jnp.concatenate(rights, axis=0))
            real = got[:BLOCK, :width] - got[BLOCK:, width:]
            imag = got[:BLOCK, width:] + got[BLOCK:, :width]
            cosine, sine = cos_sin(held_angles[at, aligned(within, BLOCK)].astype(F32) * (1.0 / ANGLE_STEPS))
            rows = aligned(start + within, BLOCK)
            wave[0, rows] = real * cosine - imag * sine
            wave[1, rows] = real * sine + imag * cosine

        loop(own_blocks, diffract, 4)

    def mix(at):
        parts = []
        for half in range(2):
            down = at * 16 + half * 8
            values = [
                (wave[0, aligned(one * part + down, 8)], wave[1, aligned(one * part + down, 8)])
                for one in range(RADIX)
            ]
            parts.append(butterfly(values, 1))
        for one in range(RADIX):
            real, imag = (jnp.concatenate([parts[0][one][c], parts[1][one][c]], axis=0) for c in range(2))
            mixed[one, aligned(at * 16, 16)] = jnp.concatenate([real, imag], axis=1).astype(BF16)

    loop(part // 16, mix)
    for group in range(cols_at):
        table_copies[group].wait()

        def fold(first, group=group):
            at = group * firsts + first
            got = dot(held_tables[0][at], mixed[at])
            real = (got[:part, :width] - got[part:, width:]).astype(BF16)
            imag = (got[:part, width:] + got[part:, :width]).astype(BF16)
            held_out[:, group, first, 0] = real.reshape(rows_at, seconds, width)
            held_out[:, group, first, 1] = imag.reshape(rows_at, seconds, width)

        loop(firsts, fold, firsts)
        fetch(held_out.at[:, group], out_ref.at[:, group])
    for copy in copies[-cols_at:]:
        copy.wait()


def column_work(later, place, shift, current, mats, angles, tables, col_count):
    peers = len(mats)
    height, width = angles[0].shape
    extent = height * peers
    part = extent // RADIX
    groups = [[current] if later else current, *mats, angles, tables if later else tables[:1]]
    counts = [len(group) for group in groups]
    sent = jax.ShapeDtypeStruct((peers, col_count, RADIX // col_count, 2, part // peers, width), BF16)
    held = sent.shape if later else (peers, 2, height, width)
    copies = sum(counts[1:-2]) + peers + (4 if later else 2) * col_count + peers

    def body(*refs):
        column_body(later, peers, counts, *refs)

    smem, anywhere = pl.BlockSpec(memory_space=pltpu.SMEM), pl.BlockSpec(memory_space=pl.ANY)
    return pl.pallas_call(
        body,
        out_shape=sent,
        in_specs=[smem, smem] + [anywhere] * sum(counts),
        out_specs=anywhere,
        scratch_shapes=[
            pltpu.VMEM((2, extent + 2 * height, width), F32),
            pltpu.VMEM((2, extent, width), F32),
            pltpu.VMEM((RADIX, part, 2 * width), BF16),
            pltpu.VMEM(held, BF16),
            pltpu.VMEM((peers, height // BLOCK, 2 * BLOCK, 3 * BLOCK), BF16),
            pltpu.VMEM((peers, height, width), angles[0].dtype),
            pltpu.VMEM(sent.shape, BF16),
            *[pltpu.VMEM(table.shape, BF16) for table in groups[-1]],
            pltpu.SemaphoreType.DMA((copies,)),
        ],
        compiler_params=params(),
        name="column_later" if later else "column_first",
    )(place, shift, *[one for group in groups for one in group])


def row_mix(order, in_ref, turn_ref, mixed, arrived):
    blocks, firsts, _, seconds, lanes = in_ref.shape
    radix, _, _, part = mixed.shape
    tiles = part // lanes

    def one_first(first):
        for tile in range(tiles):
            across = pl.ds(tile * lanes, lanes)
            for at in range(0, seconds, 16):
                values = [
                    (
                        in_ref[order[one * tiles + tile], first, 0, pl.ds(at, 16)].astype(F32),
                        in_ref[order[one * tiles + tile], first, 1, pl.ds(at, 16)].astype(F32),
                    )
                    for one in range(radix)
                ]
                for one, (real, imag) in enumerate(butterfly(values, 1)):
                    cosine, sine = turn_ref[one, 0, :, across], turn_ref[one, 1, :, across]
                    down = first * seconds + at
                    mixed[one, 0, pl.ds(down, 16), across] = (real * cosine - imag * sine).astype(BF16)
                    mixed[one, 1, pl.ds(down, 16), across] = (real * sine + imag * cosine).astype(BF16)

    for first in range(firsts):
        arrived(first)
        one_first(first)


def core_dot(left, tile_ref, sign):
    count, _, rows, depth = left.shape
    lanes = tile_ref.shape[1] // 2
    got = dot(left.reshape(count * 2 * rows, depth), tile_ref).reshape(count, 2, rows, 2 * lanes)
    first, second = got[:, 0], got[:, 1]
    if sign > 0:
        return first[..., :lanes] - second[..., lanes:], second[..., :lanes] + first[..., lanes:]
    return first[..., :lanes] + second[..., lanes:], second[..., :lanes] - first[..., lanes:]


def row_body(order, in_any, mask_any, core_any, turn_ref, out_any, mixed, passed, back, in_ref, mask_ref, core_ref, out_ref, sems):
    blocks, firsts, _, seconds, lanes = in_ref.shape
    copies = [pltpu.make_async_copy(in_any.at[:, one], in_ref.at[:, one], sems.at[one]) for one in range(firsts)]
    copies.append(pltpu.make_async_copy(core_any, core_ref, sems.at[firsts]))
    copies.append(pltpu.make_async_copy(mask_any, mask_ref, sems.at[firsts + 1]))
    for copy in copies:
        copy.start()
    radix, _, _, part = mixed.shape
    tiles = part // lanes
    rows = firsts * seconds
    row_mix(order, in_ref, turn_ref, mixed, lambda first: copies[first].wait())
    at_once = min(GROUP, radix)
    copies[firsts].wait()
    copies[firsts + 1].wait()

    for group in range(0, radix, at_once):
        these = pl.ds(group, at_once)

        def forward(tile, these=these):
            real, imag = core_dot(mixed[these], core_ref[tile], 1)
            kept = mask_ref[tile, these].astype(F32)
            across = aligned(tile * lanes, lanes)
            passed[these, 0, :, across] = (real * kept).astype(BF16)
            passed[these, 1, :, across] = (imag * kept).astype(BF16)

        loop(tiles, forward, tiles)

        def backward(tile, these=these):
            real, imag = core_dot(passed[these], core_ref[tile], -1)
            across = aligned(tile * lanes, lanes)
            cosine, sine = turn_ref[these, 0, :, across], turn_ref[these, 1, :, across]
            back[these, 0, :, across] = real * cosine + imag * sine
            back[these, 1, :, across] = imag * cosine - real * sine

        loop(tiles, backward, tiles)

    def close(first):
        for tile in range(tiles):
            across = pl.ds(tile * lanes, lanes)
            for at in range(0, seconds, 16):
                down = pl.ds(first * seconds + at, 16)
                values = [(back[one, 0, down, across], back[one, 1, down, across]) for one in range(radix)]
                for one, (real, imag) in enumerate(butterfly(values, -1)):
                    out_ref[order[one * tiles + tile], first, 0, pl.ds(at, 16)] = real.astype(BF16)
                    out_ref[order[one * tiles + tile], first, 1, pl.ds(at, 16)] = imag.astype(BF16)

    back_copies = []
    for first in range(firsts):
        close(first)
        copy = pltpu.make_async_copy(out_ref.at[:, first], out_any.at[:, first], sems.at[firsts + 2 + first])
        copy.start()
        back_copies.append(copy)
    for copy in back_copies:
        copy.wait()


def row_work(order, received, mask, tables):
    blocks, firsts, _, seconds, lanes = received.shape
    core, turns = tables
    radix, part = turns.shape[0], core.shape[1]
    rows = firsts * seconds

    anywhere = pl.BlockSpec(memory_space=pl.ANY)

    def body(*refs):
        row_body(order, *refs)

    return pl.pallas_call(
        body,
        out_shape=jax.ShapeDtypeStruct(received.shape, BF16),
        in_specs=[anywhere, anywhere, anywhere, vmem(1)[0]],
        out_specs=anywhere,
        scratch_shapes=[
            pltpu.VMEM((radix, 2, rows, part), BF16),
            pltpu.VMEM((radix, 2, rows, part), BF16),
            pltpu.VMEM((radix, 2, rows, part), F32),
            *[pltpu.VMEM(one.shape, BF16) for one in (received, mask, core, received)],
            pltpu.SemaphoreType.DMA((2 * firsts + 2,)),
        ],
        compiler_params=params(),
        name="row_both",
    )(received, mask, core, turns)


def last_row_body(order, number, place_ref, in_any, core_any, turn_ref, *refs):
    outs, (mixed, in_ref, core_ref, sems) = refs[:-4], refs[-4:]
    firsts, seconds = in_ref.shape[1], in_ref.shape[3]
    these = pl.ds(number * seconds, seconds)
    copies = [
        pltpu.make_async_copy(in_any.at[:, one, :, these], in_ref.at[:, one], sems.at[one]) for one in range(firsts)
    ]
    copies.append(pltpu.make_async_copy(core_any, core_ref, sems.at[firsts]))
    for copy in copies:
        copy.start()
    radix = mixed.shape[0]
    at_once = min(GROUP, radix)
    row_mix(order, in_ref, turn_ref, mixed, lambda first: copies[first].wait())
    copies[firsts].wait()
    for group in range(0, radix, at_once):
        these = pl.ds(group, at_once)
        for distance, out_ref in enumerate(outs):
            real, imag = core_dot(mixed[these], core_ref[place_ref[0] ^ distance], 1)
            out_ref[0, these] = real.astype(BF16)
            out_ref[1, these] = imag.astype(BF16)


def last_row_work(order, place, received, tables, number, chunks):
    blocks, firsts, _, seconds, lanes = received.shape
    core, turns = tables
    radix, part = turns.shape[0], core.shape[1]
    seconds //= chunks
    rows = firsts * seconds

    def body(*refs):
        last_row_body(order, number, *refs)

    def whole(array):
        return pl.BlockSpec(array.shape, lambda i: (0,) * array.ndim)

    anywhere = pl.BlockSpec(memory_space=pl.ANY)
    sent = jax.ShapeDtypeStruct((2, radix, rows, lanes), BF16)
    return pl.pallas_call(
        body,
        grid=(1,),
        out_shape=[sent] * (part // lanes),
        in_specs=[pl.BlockSpec(memory_space=pltpu.SMEM), anywhere, anywhere, whole(turns)],
        out_specs=[whole(sent)] * (part // lanes),
        scratch_shapes=[
            pltpu.VMEM((radix, 2, rows, part), BF16),
            pltpu.VMEM((blocks, firsts, 2, seconds, lanes), BF16),
            pltpu.VMEM(core.shape, BF16),
            pltpu.SemaphoreType.DMA((firsts + 1,)),
        ],
        compiler_params=params(),
        cost_estimate=pl.CostEstimate(flops=8 * rows * part * part * radix, bytes_accessed=2**22, transcendentals=0),
        name="row_last",
    )(place, received, core, turns)


def mask_body(in_ref, down_ref, across_ref, out_ref):
    groups, radix, rows, lanes = out_ref.shape
    turned = dot(down_ref[...], in_ref[...].astype(BF16)).astype(BF16)
    for tile in range(0, radix * lanes, 256):
        got = dot(turned, across_ref[:, tile : tile + 256]).astype(BF16)
        for within in range(0, 256, lanes):
            out_ref[:, (tile + within) // lanes] = got[:, within : within + lanes].reshape(groups, rows, lanes)


def mask_work(transmission, row_count, col_count, radix):
    height, width = transmission.shape
    down = regroup(height, RADIX).T
    across = regroup(width, radix)
    return pl.pallas_call(
        mask_body,
        out_shape=jax.ShapeDtypeStruct((col_count, radix, height // col_count, width // radix), BF16),
        in_specs=vmem(3),
        out_specs=vmem(1)[0],
        compiler_params=params(),
        name="mask_order",
    )(transmission, jnp.asarray(down), jnp.asarray(across))


def closing_body(groups, place_ref, *refs):
    given, (keep_ref, down_ref, across_ref), (out_ref, joined, turned) = refs[:groups], refs[groups : groups + 3], refs[-3:]
    _, radix, rows, lanes = given[0].shape
    for distance in range(groups):
        down = aligned((place_ref[0] ^ distance) * rows, rows)
        for number in range(2):
            for at in range(radix):
                joined[number, down, pl.ds(at * lanes, lanes)] = given[distance][number, at]
    for number in range(2):
        turned[number] = dot(down_ref[...], joined[number]).astype(BF16)
        for tile in range(0, radix * lanes, 256):
            across = pl.ds(tile, 256)
            out_ref[number, :, across] = dot(turned[number], across_ref[:, across]) * keep_ref[:, across]


def closing_work(place, received, transmission, earlier, number, chunks):
    groups = len(received)
    _, radix, rows, lanes = received[0].shape
    height, width = transmission.shape
    height //= chunks
    down = jnp.asarray(regroup(height, RADIX))
    across = jnp.asarray(regroup(width, radix).T)

    def body(*refs):
        closing_body(groups, *refs[: groups + 4], *refs[-3:])

    def whole(array):
        return pl.BlockSpec(array.shape, lambda i: (0,) * array.ndim)

    in_specs = [pl.BlockSpec(memory_space=pltpu.SMEM)] + [whole(one) for one in received]
    in_specs += [pl.BlockSpec((height, width), lambda i: (number, 0)), whole(down), whole(across)]
    arguments = [place, *received, transmission, down, across]
    aliases = {}
    if earlier is not None:
        aliases = {len(arguments): 0}
        in_specs.append(pl.BlockSpec(memory_space=pl.ANY))
        arguments.append(earlier)
    return pl.pallas_call(
        body,
        grid=(1,),
        out_shape=jax.ShapeDtypeStruct((2, height * chunks, width), F32),
        in_specs=in_specs,
        out_specs=pl.BlockSpec((2, height, width), lambda i: (0, number, 0)),
        scratch_shapes=[pltpu.VMEM((2, height, width), BF16), pltpu.VMEM((2, height, width), BF16)],
        input_output_aliases=aliases,
        compiler_params=params(),
        cost_estimate=pl.CostEstimate(flops=4 * height * width * width, bytes_accessed=2**22, transcendentals=0),
        name="closing_order",
    )(*arguments)


def exchange(value, axis):
    return lax.all_to_all(value, axis, split_axis=0, concat_axis=0, tiled=True)


def swap(value, axis, distance):
    if distance == 0:
        return value
    return lax.ppermute(value, axis, [(at, at ^ distance) for at in range(lax.axis_size(axis))])


def widen(value):
    short = -value.shape[-1] % LANES
    return jnp.pad(value, [(0, 0)] * (value.ndim - 1) + [(0, short)]) if short else value


def after(value, earlier):
    return lax.optimization_barrier((value, earlier))[0]


def gather_mats(mats):
    peers = lax.axis_size("rows")
    if peers != 8:
        result = [[swap(mats, "rows", distance)] for distance in range(peers)]
        return result, result[1]
    half = mats.shape[0] // 2
    by_x, by_y = swap(mats, "rows", 2), swap(mats, "rows", 4)
    across = [swap(by_x[:half], "rows", 4), swap(by_y[half:], "rows", 2)]
    result = []
    for pieces in ([mats], [by_x], [by_y], across):
        result += [pieces, [swap(piece, "rows", 1) for piece in pieces]]
    return result, (by_x, by_y)


def spread(value, width):
    peers, along = lax.axis_size("rows"), lax.axis_index("rows")
    chips = []
    for distance in range(0, peers, 2):
        start = ((along ^ distance) // 2) * (2 * width)
        piece = lax.dynamic_slice_in_dim(value, start, 2 * width, value.ndim - 1)
        chips.append(swap(piece, "rows", distance))

    def part(piece, core):
        return lax.dynamic_slice_in_dim(piece, core * width, width, value.ndim - 1)

    core = along % 2
    other = swap(jnp.stack([part(piece, 1 - core) for piece in chips]), "rows", 1)
    return [widen(part(piece, core)) for piece in chips] + [widen(other)]


def on_device(spectrum, diffraction, order_mask, phases, transmission, shifts):
    height, wide = spectrum.shape[1:]
    row_count, col_count = lax.axis_size("rows"), lax.axis_size("cols")
    devices = row_count * col_count
    full_rows, full_cols = height * row_count, wide * col_count
    width = wide // row_count
    part = LANES * col_count
    radix = full_cols // part
    forward, backward = column_tables(full_rows)
    column_all = (jnp.asarray(forward), jnp.asarray(backward))
    core, turns = row_tables(full_cols, part)
    row_all = (jnp.asarray(core), jnp.asarray(turns))

    along, above = lax.axis_index("rows"), lax.axis_index("cols")
    place_rows, place_cols = (at.astype(jnp.int32).reshape(1) for at in (along, above))

    masked = diffraction * order_mask.astype(BF16)[None, :, :, None, None]
    blocks = height // BLOCK
    masked = masked.transpose(1, 0, 3, 2, 4).reshape(blocks, 2 * BLOCK, 3 * BLOCK)
    mats, first_mats = gather_mats(masked)
    current = spread(spectrum, width)
    codes = jnp.round(phases * ANGLE_STEPS).astype(jnp.int16)
    angles = [spread(codes[0], width), spread(codes[1], width)]
    kept = exchange(mask_work(transmission, row_count, col_count, radix), "cols")

    narrow = width < LANES
    tiles = full_cols // LANES
    if narrow:
        order = list(range(tiles))
    else:
        order = [(at % row_count) * col_count + at // row_count for at in range(tiles)]

    def to_rows(value):
        got = exchange(value[..., :width].reshape(devices, *value.shape[2:-1], width), ("rows", "cols"))
        if not narrow:
            return got
        joined = LANES // width
        got = got.reshape(row_count, col_count, *got.shape[1:]).swapaxes(0, 1).reshape(tiles, joined, *got.shape[1:])
        return jnp.moveaxis(got, 1, -2).reshape(tiles, *got.shape[2:-1], LANES)

    def to_columns(value):
        if narrow:
            joined = LANES // width
            value = jnp.moveaxis(value.reshape(*value.shape[:-1], joined, width), -2, 1)
            value = value.reshape(col_count, row_count, *value.shape[2:]).swapaxes(0, 1)
            value = value.reshape(devices, *value.shape[2:])
        got = exchange(value, ("rows", "cols"))
        return widen(got.reshape(row_count, col_count, *got.shape[1:]))

    for bounce in range(BOUNCES):
        sent = column_work(
            bounce > 0, place_rows, shifts[bounce : bounce + 1], current, mats, angles[bounce], column_all, col_count
        )
        received = to_rows(sent)
        if bounce < BOUNCES - 1:
            current = to_columns(row_work(order, received, kept, row_all))
    chunks = 2 if received.shape[3] % 32 == 0 else 1
    worked = [last_row_work(order, place_cols, received, row_all, number, chunks) for number in range(chunks)]
    worked = [[swap(one, "cols", distance) for distance, one in enumerate(chunk)] for chunk in worked]
    outgoing = None
    for number in range(chunks):
        outgoing = closing_work(place_cols, worked[number], transmission, outgoing, number, chunks)
    return outgoing


def solution(mesh):
    placed = (
        P(None, "rows", "cols"),
        P(None, "rows", None, None, None),
        P("rows", None),
        P(None, "rows", "cols"),
        P("rows", "cols"),
        P(),
    )
    return jax.shard_map(
        on_device, mesh=mesh, in_specs=placed, out_specs=P(None, "rows", "cols"), check_vma=False
    )
```

```python
import math

import jax
import jax.numpy as jnp
import ml_dtypes
import numpy as np
from jax import lax
from jax.experimental import pallas as pl
from jax.experimental.pallas import tpu as pltpu
from jax.sharding import PartitionSpec as P

BLOCK = 128
LANES = 128
RADIX = 16
BOUNCES = 2
GROUP = 4
ANGLE_STEPS = 10430.0
VMEM_LIMIT = 62 * 1024 * 1024
BF16 = jnp.bfloat16
F32 = jnp.float32


def params(limit=VMEM_LIMIT):
    return pltpu.CompilerParams(vmem_limit_bytes=limit)


def vmem(count):
    return [pl.BlockSpec(memory_space=pltpu.VMEM) for _ in range(count)]


def column_tables(extent):
    part = extent // RADIX
    first = np.arange(RADIX)[:, None, None]
    second = np.arange(part)[None, :, None]
    inner = np.arange(part)[None, None, :]
    angle = ((first + RADIX * second) * inner % extent) * (2.0 * np.pi / extent)
    scale = 1.0 / math.sqrt(extent)
    real, imag = np.cos(angle) * scale, np.sin(angle) * scale
    forward = np.concatenate([real, imag], axis=1)
    backward = np.concatenate([real.transpose(0, 2, 1), imag.transpose(0, 2, 1)], axis=1)
    return forward.astype(ml_dtypes.bfloat16), backward.astype(ml_dtypes.bfloat16)


def row_tables(extent, part):
    radix = extent // part
    inner = np.arange(part)
    angle = (inner[:, None] * inner[None, :] % part) * (2.0 * np.pi / part)
    scale = 1.0 / math.sqrt(extent)
    core = np.stack([np.cos(angle) * scale, np.sin(angle) * scale], axis=1)
    core = core.reshape(part, 2, part // LANES, LANES).transpose(2, 0, 1, 3).reshape(part // LANES, part, 2 * LANES)
    turn = (np.arange(radix)[:, None] * inner[None, :]) * (2.0 * np.pi / extent)
    turns = np.stack([np.cos(turn), np.sin(turn)], axis=1)[:, :, None, :]
    return core.astype(ml_dtypes.bfloat16), turns.astype(np.float32)


def regroup(count, fast):
    natural = np.arange(count)
    grouped = (natural % fast) * (count // fast) + natural // fast
    matrix = np.zeros((count, count), np.float32)
    matrix[natural, grouped] = 1.0
    return matrix.astype(ml_dtypes.bfloat16)


def half_series():
    top = (np.pi / 2) ** 2
    squares = (np.polynomial.chebyshev.chebpts1(200) + 1) * (top / 2)
    angles = np.sqrt(squares)

    def fit(values):
        series = np.polynomial.chebyshev.Chebyshev.fit(squares, values, 4, domain=[0, top])
        return [float(c) for c in series.convert(kind=np.polynomial.Polynomial).coef]

    return fit(np.sin(angles) / angles), fit(np.cos(angles))


SINE_SERIES, COSINE_SERIES = half_series()


def cos_sin(angle):
    half = angle * 0.5
    square = half * half

    def series(coefs):
        total = square * coefs[-1] + coefs[-2]
        for coef in coefs[-3::-1]:
            total = total * square + coef
        return total

    twice_sine, cosine = angle * series(SINE_SERIES), series(COSINE_SERIES)
    return 1.0 - twice_sine * twice_sine * 0.5, twice_sine * cosine


def butterfly(values, sign):
    count = len(values)
    if count == 1:
        return values
    even, odd = butterfly(values[0::2], sign), butterfly(values[1::2], sign)
    low, high = [], []
    for at in range(count // 2):
        real, imag = odd[at]
        if at == 0:
            turned = real, imag
        elif 4 * at == count:
            turned = (-imag, real) if sign > 0 else (imag, -real)
        elif 8 * at == count:
            half = math.sqrt(0.5)
            turned = (
                ((real - imag) * half, (real + imag) * half)
                if sign > 0
                else ((real + imag) * half, (imag - real) * half)
            )
        elif 8 * at == 3 * count:
            half = math.sqrt(0.5)
            turned = (
                ((real + imag) * -half, (real - imag) * half)
                if sign > 0
                else ((imag - real) * half, (real + imag) * -half)
            )
        else:
            cosine = math.cos(2 * math.pi * at / count)
            sine = sign * math.sin(2 * math.pi * at / count)
            turned = real * cosine - imag * sine, real * sine + imag * cosine
        low.append((even[at][0] + turned[0], even[at][1] + turned[1]))
        high.append((even[at][0] - turned[0], even[at][1] - turned[1]))
    return low + high


def dot(left, right):
    return jnp.dot(left, right, preferred_element_type=F32)


def loop(count, body, unroll=1):
    def step(at, carry):
        body(at)
        return carry

    lax.fori_loop(0, count, step, 0, unroll=min(unroll, count))


def aligned(start, size):
    return pl.ds(pl.multiple_of(start, size), size)


def by_distance(pieces, distance):
    return pieces[-1].at[distance // 2] if distance % 2 else pieces[distance // 2]


def column_body(later, peers, counts, *refs):
    (place_ref, shift_ref), refs = refs[:2], refs[2:]
    groups = []
    for count in counts:
        groups.append(refs[:count])
        refs = refs[count:]
    current, *mats, angles, tables = groups
    out_ref, padded, wave, mixed, held_current, held_mats, held_angles, held_out = refs[:8]
    held_tables, sems = refs[8:-1], refs[-1]
    rows_at, cols_at, firsts, _, seconds, width = out_ref.shape
    extent = wave.shape[1]
    part = extent // RADIX
    height = extent // peers
    own_blocks = height // BLOCK

    copies = []

    def fetch(source, target):
        copy = pltpu.make_async_copy(source, target, sems.at[len(copies)])
        copy.start()
        copies.append(copy)
        return copy

    def fetch_table(number, group):
        mine = pl.ds(group * firsts, firsts)
        return fetch(tables[number].at[mine], held_tables[number].at[mine])

    if later:
        current_copies = []
        for group in range(cols_at):
            some = [fetch(current[0].at[:, group], held_current.at[:, group]), fetch_table(1, group)]
            current_copies.append(some)
    else:
        current_copies = [
            fetch(by_distance(current, at), held_current.at[at]) for at in range(peers)
        ]
    mat_copies, angle_copies = [], []
    for at in range(peers):
        first, some = 0, []
        for piece in mats[at]:
            some.append(fetch(piece, held_mats.at[at, pl.ds(first, piece.shape[0])]))
            first += piece.shape[0]
        mat_copies.append(some)
        angle_copies.append(fetch(by_distance(angles, at), held_angles.at[at]))
    table_copies = [fetch_table(0, group) for group in range(cols_at)]

    padded[:, pl.ds(0, height)] = jnp.zeros((2, height, width), F32)
    padded[:, pl.ds(height + extent, height)] = jnp.zeros((2, height, width), F32)

    if later:
        for group in range(cols_at):
            for copy in current_copies[group]:
                copy.wait()

            def unfold(first, group=group):
                at = group * firsts + first
                real = held_current[:, group, first, 0].reshape(part, width)
                imag = held_current[:, group, first, 1].reshape(part, width)
                got = dot(held_tables[-1][at], jnp.concatenate([real, imag], axis=1))
                rows = aligned(at * part, part)
                wave[0, rows] = got[:part, :width] + got[part:, width:]
                wave[1, rows] = got[:part, width:] - got[part:, :width]

            loop(firsts, unfold, firsts)

        def gather(at):
            values = [
                (wave[0, aligned(one * part + at * 8, 8)], wave[1, aligned(one * part + at * 8, 8)])
                for one in range(RADIX)
            ]
            for one, (real, imag) in enumerate(butterfly(values, -1)):
                rows = aligned(height + one * part + at * 8, 8)
                padded[0, rows] = real
                padded[1, rows] = imag

        loop(part // 8, gather, 2)
    else:
        for at in range(peers):
            rows = aligned(height + (place_ref[0] ^ at) * height, height)
            current_copies[at].wait()
            padded[0, rows] = held_current[at, 0].astype(F32)
            padded[1, rows] = held_current[at, 1].astype(F32)

    shift = shift_ref[0]
    for at in range(peers):
        start = (place_ref[0] ^ at) * height
        for copy in mat_copies[at]:
            copy.wait()
        angle_copies[at].wait()

        def diffract(block, at=at, start=start):
            within = block * BLOCK
            rights = []
            for order in range(3):
                rows = pl.ds(height + start + within + (order - 1) * shift, BLOCK)
                rights.append(jnp.concatenate([padded[0, rows], padded[1, rows]], axis=1).astype(BF16))
            got = dot(held_mats[at, block], jnp.concatenate(rights, axis=0))
            real = got[:BLOCK, :width] - got[BLOCK:, width:]
            imag = got[:BLOCK, width:] + got[BLOCK:, :width]
            cosine, sine = cos_sin(held_angles[at, aligned(within, BLOCK)].astype(F32) * (1.0 / ANGLE_STEPS))
            rows = aligned(start + within, BLOCK)
            wave[0, rows] = real * cosine - imag * sine
            wave[1, rows] = real * sine + imag * cosine

        loop(own_blocks, diffract, 4)

    def mix(at):
        parts = []
        for half in range(2):
            down = at * 16 + half * 8
            values = [
                (wave[0, aligned(one * part + down, 8)], wave[1, aligned(one * part + down, 8)])
                for one in range(RADIX)
            ]
            parts.append(butterfly(values, 1))
        for one in range(RADIX):
            real, imag = (jnp.concatenate([parts[0][one][c], parts[1][one][c]], axis=0) for c in range(2))
            mixed[one, aligned(at * 16, 16)] = jnp.concatenate([real, imag], axis=1).astype(BF16)

    loop(part // 16, mix)
    for group in range(cols_at):
        table_copies[group].wait()

        def fold(first, group=group):
            at = group * firsts + first
            got = dot(held_tables[0][at], mixed[at])
            real = (got[:part, :width] - got[part:, width:]).astype(BF16)
            imag = (got[:part, width:] + got[part:, :width]).astype(BF16)
            held_out[:, group, first, 0] = real.reshape(rows_at, seconds, width)
            held_out[:, group, first, 1] = imag.reshape(rows_at, seconds, width)

        loop(firsts, fold, firsts)
        fetch(held_out.at[:, group], out_ref.at[:, group])
    for copy in copies[-cols_at:]:
        copy.wait()


def column_work(later, place, shift, current, mats, angles, tables, col_count):
    peers = len(mats)
    height, width = angles[0].shape
    extent = height * peers
    part = extent // RADIX
    groups = [[current] if later else current, *mats, angles, tables if later else tables[:1]]
    counts = [len(group) for group in groups]
    sent = jax.ShapeDtypeStruct((peers, col_count, RADIX // col_count, 2, part // peers, width), BF16)
    held = sent.shape if later else (peers, 2, height, width)
    copies = sum(counts[1:-2]) + peers + (4 if later else 2) * col_count + peers

    def body(*refs):
        column_body(later, peers, counts, *refs)

    smem, anywhere = pl.BlockSpec(memory_space=pltpu.SMEM), pl.BlockSpec(memory_space=pl.ANY)
    return pl.pallas_call(
        body,
        out_shape=sent,
        in_specs=[smem, smem] + [anywhere] * sum(counts),
        out_specs=anywhere,
        scratch_shapes=[
            pltpu.VMEM((2, extent + 2 * height, width), F32),
            pltpu.VMEM((2, extent, width), F32),
            pltpu.VMEM((RADIX, part, 2 * width), BF16),
            pltpu.VMEM(held, BF16),
            pltpu.VMEM((peers, height // BLOCK, 2 * BLOCK, 3 * BLOCK), BF16),
            pltpu.VMEM((peers, height, width), angles[0].dtype),
            pltpu.VMEM(sent.shape, BF16),
            *[pltpu.VMEM(table.shape, BF16) for table in groups[-1]],
            pltpu.SemaphoreType.DMA((copies,)),
        ],
        compiler_params=params(),
        name="column_later" if later else "column_first",
    )(place, shift, *[one for group in groups for one in group])


def row_mix(order, in_ref, turn_ref, mixed, arrived):
    blocks, firsts, _, seconds, lanes = in_ref.shape
    radix, _, _, part = mixed.shape
    tiles = part // lanes

    def one_first(first):
        for tile in range(tiles):
            across = pl.ds(tile * lanes, lanes)
            for at in range(0, seconds, 16):
                values = [
                    (
                        in_ref[order[one * tiles + tile], first, 0, pl.ds(at, 16)].astype(F32),
                        in_ref[order[one * tiles + tile], first, 1, pl.ds(at, 16)].astype(F32),
                    )
                    for one in range(radix)
                ]
                for one, (real, imag) in enumerate(butterfly(values, 1)):
                    cosine, sine = turn_ref[one, 0, :, across], turn_ref[one, 1, :, across]
                    down = first * seconds + at
                    mixed[one, 0, pl.ds(down, 16), across] = (real * cosine - imag * sine).astype(BF16)
                    mixed[one, 1, pl.ds(down, 16), across] = (real * sine + imag * cosine).astype(BF16)

    for first in range(firsts):
        arrived(first)
        one_first(first)


def core_dot(left, tile_ref, sign):
    count, _, rows, depth = left.shape
    lanes = tile_ref.shape[1] // 2
    got = dot(left.reshape(count * 2 * rows, depth), tile_ref).reshape(count, 2, rows, 2 * lanes)
    first, second = got[:, 0], got[:, 1]
    if sign > 0:
        return first[..., :lanes] - second[..., lanes:], second[..., :lanes] + first[..., lanes:]
    return first[..., :lanes] + second[..., lanes:], second[..., :lanes] - first[..., lanes:]


def row_body(order, in_any, mask_any, core_any, turn_ref, out_any, mixed, passed, back, in_ref, mask_ref, core_ref, out_ref, sems):
    blocks, firsts, _, seconds, lanes = in_ref.shape
    copies = [pltpu.make_async_copy(in_any.at[:, one], in_ref.at[:, one], sems.at[one]) for one in range(firsts)]
    copies.append(pltpu.make_async_copy(core_any, core_ref, sems.at[firsts]))
    copies.append(pltpu.make_async_copy(mask_any, mask_ref, sems.at[firsts + 1]))
    for copy in copies:
        copy.start()
    radix, _, _, part = mixed.shape
    tiles = part // lanes
    rows = firsts * seconds
    row_mix(order, in_ref, turn_ref, mixed, lambda first: copies[first].wait())
    at_once = min(GROUP, radix)
    copies[firsts].wait()
    copies[firsts + 1].wait()

    for group in range(0, radix, at_once):
        these = pl.ds(group, at_once)

        def forward(tile, these=these):
            real, imag = core_dot(mixed[these], core_ref[tile], 1)
            kept = mask_ref[tile, these].astype(F32)
            across = aligned(tile * lanes, lanes)
            passed[these, 0, :, across] = (real * kept).astype(BF16)
            passed[these, 1, :, across] = (imag * kept).astype(BF16)

        loop(tiles, forward, tiles)

        def backward(tile, these=these):
            real, imag = core_dot(passed[these], core_ref[tile], -1)
            across = aligned(tile * lanes, lanes)
            cosine, sine = turn_ref[these, 0, :, across], turn_ref[these, 1, :, across]
            back[these, 0, :, across] = real * cosine + imag * sine
            back[these, 1, :, across] = imag * cosine - real * sine

        loop(tiles, backward, tiles)

    def close(first):
        for tile in range(tiles):
            across = pl.ds(tile * lanes, lanes)
            for at in range(0, seconds, 16):
                down = pl.ds(first * seconds + at, 16)
                values = [(back[one, 0, down, across], back[one, 1, down, across]) for one in range(radix)]
                for one, (real, imag) in enumerate(butterfly(values, -1)):
                    out_ref[order[one * tiles + tile], first, 0, pl.ds(at, 16)] = real.astype(BF16)
                    out_ref[order[one * tiles + tile], first, 1, pl.ds(at, 16)] = imag.astype(BF16)

    back_copies = []
    for first in range(firsts):
        close(first)
        copy = pltpu.make_async_copy(out_ref.at[:, first], out_any.at[:, first], sems.at[firsts + 2 + first])
        copy.start()
        back_copies.append(copy)
    for copy in back_copies:
        copy.wait()


def row_work(order, received, mask, tables):
    blocks, firsts, _, seconds, lanes = received.shape
    core, turns = tables
    radix, part = turns.shape[0], core.shape[1]
    rows = firsts * seconds

    anywhere = pl.BlockSpec(memory_space=pl.ANY)

    def body(*refs):
        row_body(order, *refs)

    return pl.pallas_call(
        body,
        out_shape=jax.ShapeDtypeStruct(received.shape, BF16),
        in_specs=[anywhere, anywhere, anywhere, vmem(1)[0]],
        out_specs=anywhere,
        scratch_shapes=[
            pltpu.VMEM((radix, 2, rows, part), BF16),
            pltpu.VMEM((radix, 2, rows, part), BF16),
            pltpu.VMEM((radix, 2, rows, part), F32),
            *[pltpu.VMEM(one.shape, BF16) for one in (received, mask, core, received)],
            pltpu.SemaphoreType.DMA((2 * firsts + 2,)),
        ],
        compiler_params=params(),
        name="row_both",
    )(received, mask, core, turns)


def last_row_body(order, number, place_ref, in_any, core_any, turn_ref, *refs):
    outs, (mixed, in_ref, core_ref, sems) = refs[:-4], refs[-4:]
    firsts, seconds = in_ref.shape[1], in_ref.shape[3]
    these = pl.ds(number * seconds, seconds)
    copies = [
        pltpu.make_async_copy(in_any.at[:, one, :, these], in_ref.at[:, one], sems.at[one]) for one in range(firsts)
    ]
    copies.append(pltpu.make_async_copy(core_any, core_ref, sems.at[firsts]))
    for copy in copies:
        copy.start()
    radix = mixed.shape[0]
    at_once = min(GROUP, radix)
    row_mix(order, in_ref, turn_ref, mixed, lambda first: copies[first].wait())
    copies[firsts].wait()
    for group in range(0, radix, at_once):
        these = pl.ds(group, at_once)
        for distance, out_ref in enumerate(outs):
            real, imag = core_dot(mixed[these], core_ref[place_ref[0] ^ distance], 1)
            out_ref[0, these] = real.astype(BF16)
            out_ref[1, these] = imag.astype(BF16)


def last_row_work(order, place, received, tables, number, chunks):
    blocks, firsts, _, seconds, lanes = received.shape
    core, turns = tables
    radix, part = turns.shape[0], core.shape[1]
    seconds //= chunks
    rows = firsts * seconds

    def body(*refs):
        last_row_body(order, number, *refs)

    def whole(array):
        return pl.BlockSpec(array.shape, lambda i: (0,) * array.ndim)

    anywhere = pl.BlockSpec(memory_space=pl.ANY)
    sent = jax.ShapeDtypeStruct((2, radix, rows, lanes), BF16)
    return pl.pallas_call(
        body,
        grid=(1,),
        out_shape=[sent] * (part // lanes),
        in_specs=[pl.BlockSpec(memory_space=pltpu.SMEM), anywhere, anywhere, whole(turns)],
        out_specs=[whole(sent)] * (part // lanes),
        scratch_shapes=[
            pltpu.VMEM((radix, 2, rows, part), BF16),
            pltpu.VMEM((blocks, firsts, 2, seconds, lanes), BF16),
            pltpu.VMEM(core.shape, BF16),
            pltpu.SemaphoreType.DMA((firsts + 1,)),
        ],
        compiler_params=params(),
        cost_estimate=pl.CostEstimate(flops=8 * rows * part * part * radix, bytes_accessed=2**22, transcendentals=0),
        name="row_last",
    )(place, received, core, turns)


def mask_body(in_ref, down_ref, across_ref, out_ref):
    groups, radix, rows, lanes = out_ref.shape
    turned = dot(down_ref[...], in_ref[...].astype(BF16)).astype(BF16)
    for tile in range(0, radix * lanes, 256):
        got = dot(turned, across_ref[:, tile : tile + 256]).astype(BF16)
        for within in range(0, 256, lanes):
            out_ref[:, (tile + within) // lanes] = got[:, within : within + lanes].reshape(groups, rows, lanes)


def mask_work(transmission, row_count, col_count, radix):
    height, width = transmission.shape
    down = regroup(height, RADIX).T
    across = regroup(width, radix)
    return pl.pallas_call(
        mask_body,
        out_shape=jax.ShapeDtypeStruct((col_count, radix, height // col_count, width // radix), BF16),
        in_specs=vmem(3),
        out_specs=vmem(1)[0],
        compiler_params=params(),
        name="mask_order",
    )(transmission, jnp.asarray(down), jnp.asarray(across))


def closing_body(groups, place_ref, *refs):
    given, (keep_ref, down_ref, across_ref), (out_ref, joined, turned) = refs[:groups], refs[groups : groups + 3], refs[-3:]
    _, radix, rows, lanes = given[0].shape
    for distance in range(groups):
        down = aligned((place_ref[0] ^ distance) * rows, rows)
        for number in range(2):
            for at in range(radix):
                joined[number, down, pl.ds(at * lanes, lanes)] = given[distance][number, at]
    for number in range(2):
        turned[number] = dot(down_ref[...], joined[number]).astype(BF16)
        for tile in range(0, radix * lanes, 256):
            across = pl.ds(tile, 256)
            out_ref[number, :, across] = dot(turned[number], across_ref[:, across]) * keep_ref[:, across]


def closing_work(place, received, transmission, earlier, number, chunks):
    groups = len(received)
    _, radix, rows, lanes = received[0].shape
    height, width = transmission.shape
    height //= chunks
    down = jnp.asarray(regroup(height, RADIX))
    across = jnp.asarray(regroup(width, radix).T)

    def body(*refs):
        closing_body(groups, *refs[: groups + 4], *refs[-3:])

    def whole(array):
        return pl.BlockSpec(array.shape, lambda i: (0,) * array.ndim)

    in_specs = [pl.BlockSpec(memory_space=pltpu.SMEM)] + [whole(one) for one in received]
    in_specs += [pl.BlockSpec((height, width), lambda i: (number, 0)), whole(down), whole(across)]
    arguments = [place, *received, transmission, down, across]
    aliases = {}
    if earlier is not None:
        aliases = {len(arguments): 0}
        in_specs.append(pl.BlockSpec(memory_space=pl.ANY))
        arguments.append(earlier)
    return pl.pallas_call(
        body,
        grid=(1,),
        out_shape=jax.ShapeDtypeStruct((2, height * chunks, width), F32),
        in_specs=in_specs,
        out_specs=pl.BlockSpec((2, height, width), lambda i: (0, number, 0)),
        scratch_shapes=[pltpu.VMEM((2, height, width), BF16), pltpu.VMEM((2, height, width), BF16)],
        input_output_aliases=aliases,
        compiler_params=params(24 * 1024 * 1024),
        cost_estimate=pl.CostEstimate(flops=4 * height * width * width, bytes_accessed=2**22, transcendentals=0),
        name="closing_order",
    )(*arguments)


def exchange(value, axis):
    return lax.all_to_all(value, axis, split_axis=0, concat_axis=0, tiled=True)


def swap(value, axis, distance):
    if distance == 0:
        return value
    return lax.ppermute(value, axis, [(at, at ^ distance) for at in range(lax.axis_size(axis))])


def widen(value):
    short = -value.shape[-1] % LANES
    return jnp.pad(value, [(0, 0)] * (value.ndim - 1) + [(0, short)]) if short else value


def after(value, earlier):
    return lax.optimization_barrier((value, earlier))[0]


def gather_mats(mats):
    peers = lax.axis_size("rows")
    if peers != 8:
        result = [[swap(mats, "rows", distance)] for distance in range(peers)]
        return result, result[1]
    half = mats.shape[0] // 2
    by_x, by_y = swap(mats, "rows", 2), swap(mats, "rows", 4)
    across = [swap(by_x[:half], "rows", 4), swap(by_y[half:], "rows", 2)]
    result = []
    for pieces in ([mats], [by_x], [by_y], across):
        result += [pieces, [swap(piece, "rows", 1) for piece in pieces]]
    return result, (by_x, by_y)


def spread(value, width):
    peers, along = lax.axis_size("rows"), lax.axis_index("rows")
    chips = []
    for distance in range(0, peers, 2):
        start = ((along ^ distance) // 2) * (2 * width)
        piece = lax.dynamic_slice_in_dim(value, start, 2 * width, value.ndim - 1)
        chips.append(swap(piece, "rows", distance))

    def part(piece, core):
        return lax.dynamic_slice_in_dim(piece, core * width, width, value.ndim - 1)

    core = along % 2
    other = swap(jnp.stack([part(piece, 1 - core) for piece in chips]), "rows", 1)
    return [widen(part(piece, core)) for piece in chips] + [widen(other)]


def on_device(spectrum, diffraction, order_mask, phases, transmission, shifts):
    height, wide = spectrum.shape[1:]
    row_count, col_count = lax.axis_size("rows"), lax.axis_size("cols")
    devices = row_count * col_count
    full_rows, full_cols = height * row_count, wide * col_count
    width = wide // row_count
    part = LANES * col_count
    radix = full_cols // part
    forward, backward = column_tables(full_rows)
    column_all = (jnp.asarray(forward), jnp.asarray(backward))
    core, turns = row_tables(full_cols, part)
    row_all = (jnp.asarray(core), jnp.asarray(turns))

    along, above = lax.axis_index("rows"), lax.axis_index("cols")
    place_rows, place_cols = (at.astype(jnp.int32).reshape(1) for at in (along, above))

    masked = diffraction * order_mask.astype(BF16)[None, :, :, None, None]
    blocks = height // BLOCK
    masked = masked.transpose(1, 0, 3, 2, 4).reshape(blocks, 2 * BLOCK, 3 * BLOCK)
    mats, first_mats = gather_mats(masked)
    current = spread(spectrum, width)
    codes = jnp.round(phases * ANGLE_STEPS).astype(jnp.int16)
    angles = [spread(codes[0], width), spread(codes[1], width)]
    kept = exchange(mask_work(transmission, row_count, col_count, radix), "cols")

    narrow = width < LANES
    tiles = full_cols // LANES
    if narrow:
        order = list(range(tiles))
    else:
        order = [(at % row_count) * col_count + at // row_count for at in range(tiles)]

    def to_rows(value):
        got = exchange(value[..., :width].reshape(devices, *value.shape[2:-1], width), ("rows", "cols"))
        if not narrow:
            return got
        joined = LANES // width
        got = got.reshape(row_count, col_count, *got.shape[1:]).swapaxes(0, 1).reshape(tiles, joined, *got.shape[1:])
        return jnp.moveaxis(got, 1, -2).reshape(tiles, *got.shape[2:-1], LANES)

    def to_columns(value):
        if narrow:
            joined = LANES // width
            value = jnp.moveaxis(value.reshape(*value.shape[:-1], joined, width), -2, 1)
            value = value.reshape(col_count, row_count, *value.shape[2:]).swapaxes(0, 1)
            value = value.reshape(devices, *value.shape[2:])
        got = exchange(value, ("rows", "cols"))
        return widen(got.reshape(row_count, col_count, *got.shape[1:]))

    for bounce in range(BOUNCES):
        sent = column_work(
            bounce > 0, place_rows, shifts[bounce : bounce + 1], current, mats, angles[bounce], column_all, col_count
        )
        received = to_rows(sent)
        if bounce < BOUNCES - 1:
            current = to_columns(row_work(order, received, kept, row_all))
    chunks = 2 if received.shape[3] % 32 == 0 else 1
    worked = [last_row_work(order, place_cols, received, row_all, number, chunks) for number in range(chunks)]
    worked = [[swap(one, "cols", distance) for distance, one in enumerate(chunk)] for chunk in worked]
    outgoing = None
    for number in range(chunks):
        outgoing = closing_work(place_cols, worked[number], transmission, outgoing, number, chunks)
    return outgoing


def solution(mesh):
    placed = (
        P(None, "rows", "cols"),
        P(None, "rows", None, None, None),
        P("rows", None),
        P(None, "rows", "cols"),
        P("rows", "cols"),
        P(),
    )
    return jax.shard_map(
        on_device, mesh=mesh, in_specs=placed, out_specs=P(None, "rows", "cols"), check_vma=False
    )
```

```python
import math

import jax
import jax.numpy as jnp
import ml_dtypes
import numpy as np
from jax import lax
from jax.experimental import pallas as pl
from jax.experimental.pallas import tpu as pltpu
from jax.sharding import PartitionSpec as P

BLOCK = 128
LANES = 128
RADIX = 16
BOUNCES = 2
GROUP = 4
ANGLE_STEPS = 10430.0
VMEM_LIMIT = 62 * 1024 * 1024
BF16 = jnp.bfloat16
F32 = jnp.float32


def params(limit=VMEM_LIMIT):
    return pltpu.CompilerParams(vmem_limit_bytes=limit)


def vmem(count):
    return [pl.BlockSpec(memory_space=pltpu.VMEM) for _ in range(count)]


def column_tables(extent):
    part = extent // RADIX
    first = np.arange(RADIX)[:, None, None]
    second = np.arange(part)[None, :, None]
    inner = np.arange(part)[None, None, :]
    angle = ((first + RADIX * second) * inner % extent) * (2.0 * np.pi / extent)
    scale = 1.0 / math.sqrt(extent)
    real, imag = np.cos(angle) * scale, np.sin(angle) * scale
    forward = np.concatenate([real, imag], axis=1)
    backward = np.concatenate([real.transpose(0, 2, 1), imag.transpose(0, 2, 1)], axis=1)
    return forward.astype(ml_dtypes.bfloat16), backward.astype(ml_dtypes.bfloat16)


def row_tables(extent, part):
    radix = extent // part
    inner = np.arange(part)
    angle = (inner[:, None] * inner[None, :] % part) * (2.0 * np.pi / part)
    scale = 1.0 / math.sqrt(extent)
    core = np.stack([np.cos(angle) * scale, np.sin(angle) * scale], axis=1)
    core = core.reshape(part, 2, part // LANES, LANES).transpose(2, 0, 1, 3).reshape(part // LANES, part, 2 * LANES)
    turn = (np.arange(radix)[:, None] * inner[None, :]) * (2.0 * np.pi / extent)
    turns = np.stack([np.cos(turn), np.sin(turn)], axis=1)[:, :, None, :]
    return core.astype(ml_dtypes.bfloat16), turns.astype(np.float32)


def regroup(count, fast):
    natural = np.arange(count)
    grouped = (natural % fast) * (count // fast) + natural // fast
    matrix = np.zeros((count, count), np.float32)
    matrix[natural, grouped] = 1.0
    return matrix.astype(ml_dtypes.bfloat16)


def half_series():
    top = (np.pi / 2) ** 2
    squares = (np.polynomial.chebyshev.chebpts1(200) + 1) * (top / 2)
    angles = np.sqrt(squares)

    def fit(values):
        series = np.polynomial.chebyshev.Chebyshev.fit(squares, values, 4, domain=[0, top])
        return [float(c) for c in series.convert(kind=np.polynomial.Polynomial).coef]

    return fit(np.sin(angles) / angles), fit(np.cos(angles))


SINE_SERIES, COSINE_SERIES = half_series()


def cos_sin(angle):
    half = angle * 0.5
    square = half * half

    def series(coefs):
        total = square * coefs[-1] + coefs[-2]
        for coef in coefs[-3::-1]:
            total = total * square + coef
        return total

    twice_sine, cosine = angle * series(SINE_SERIES), series(COSINE_SERIES)
    return 1.0 - twice_sine * twice_sine * 0.5, twice_sine * cosine


def butterfly(values, sign):
    count = len(values)
    if count == 1:
        return values
    even, odd = butterfly(values[0::2], sign), butterfly(values[1::2], sign)
    low, high = [], []
    for at in range(count // 2):
        real, imag = odd[at]
        if at == 0:
            turned = real, imag
        elif 4 * at == count:
            turned = (-imag, real) if sign > 0 else (imag, -real)
        elif 8 * at == count:
            half = math.sqrt(0.5)
            turned = (
                ((real - imag) * half, (real + imag) * half)
                if sign > 0
                else ((real + imag) * half, (imag - real) * half)
            )
        elif 8 * at == 3 * count:
            half = math.sqrt(0.5)
            turned = (
                ((real + imag) * -half, (real - imag) * half)
                if sign > 0
                else ((imag - real) * half, (real + imag) * -half)
            )
        else:
            cosine = math.cos(2 * math.pi * at / count)
            sine = sign * math.sin(2 * math.pi * at / count)
            turned = real * cosine - imag * sine, real * sine + imag * cosine
        low.append((even[at][0] + turned[0], even[at][1] + turned[1]))
        high.append((even[at][0] - turned[0], even[at][1] - turned[1]))
    return low + high


def dot(left, right):
    return jnp.dot(left, right, preferred_element_type=F32)


def loop(count, body, unroll=1):
    def step(at, carry):
        body(at)
        return carry

    lax.fori_loop(0, count, step, 0, unroll=min(unroll, count))


def aligned(start, size):
    return pl.ds(pl.multiple_of(start, size), size)


def by_distance(pieces, distance):
    return pieces[-1].at[distance // 2] if distance % 2 else pieces[distance // 2]


def column_body(later, peers, counts, *refs):
    (place_ref, shift_ref), refs = refs[:2], refs[2:]
    groups = []
    for count in counts:
        groups.append(refs[:count])
        refs = refs[count:]
    current, *mats, angles, tables = groups
    out_ref, padded, wave, mixed, held_current, held_mats, held_angles, held_out = refs[:8]
    held_tables, sems = refs[8:-1], refs[-1]
    rows_at, cols_at, firsts, _, seconds, width = out_ref.shape
    extent = wave.shape[1]
    part = extent // RADIX
    height = extent // peers
    own_blocks = height // BLOCK

    copies = []

    def fetch(source, target):
        copy = pltpu.make_async_copy(source, target, sems.at[len(copies)])
        copy.start()
        copies.append(copy)
        return copy

    def fetch_table(number, group):
        mine = pl.ds(group * firsts, firsts)
        return fetch(tables[number].at[mine], held_tables[number].at[mine])

    if later:
        current_copies = []
        for group in range(cols_at):
            some = [fetch(current[0].at[:, group], held_current.at[:, group]), fetch_table(1, group)]
            current_copies.append(some)
    else:
        current_copies = [
            fetch(by_distance(current, at), held_current.at[at]) for at in range(peers)
        ]
    mat_copies, angle_copies = [], []
    for at in range(peers):
        first, some = 0, []
        for piece in mats[at]:
            some.append(fetch(piece, held_mats.at[at, pl.ds(first, piece.shape[0])]))
            first += piece.shape[0]
        mat_copies.append(some)
        angle_copies.append(fetch(by_distance(angles, at), held_angles.at[at]))
    table_copies = [fetch_table(0, group) for group in range(cols_at)]

    padded[:, pl.ds(0, height)] = jnp.zeros((2, height, width), F32)
    padded[:, pl.ds(height + extent, height)] = jnp.zeros((2, height, width), F32)

    if later:
        for group in range(cols_at):
            for copy in current_copies[group]:
                copy.wait()

            def unfold(first, group=group):
                at = group * firsts + first
                real = held_current[:, group, first, 0].reshape(part, width)
                imag = held_current[:, group, first, 1].reshape(part, width)
                got = dot(held_tables[-1][at], jnp.concatenate([real, imag], axis=1))
                rows = aligned(at * part, part)
                wave[0, rows] = got[:part, :width] + got[part:, width:]
                wave[1, rows] = got[:part, width:] - got[part:, :width]

            loop(firsts, unfold, firsts)

        def gather(at):
            values = [
                (wave[0, aligned(one * part + at * 8, 8)], wave[1, aligned(one * part + at * 8, 8)])
                for one in range(RADIX)
            ]
            for one, (real, imag) in enumerate(butterfly(values, -1)):
                rows = aligned(height + one * part + at * 8, 8)
                padded[0, rows] = real
                padded[1, rows] = imag

        loop(part // 8, gather, 2)
    else:
        for at in range(peers):
            rows = aligned(height + (place_ref[0] ^ at) * height, height)
            current_copies[at].wait()
            padded[0, rows] = held_current[at, 0].astype(F32)
            padded[1, rows] = held_current[at, 1].astype(F32)

    shift = shift_ref[0]
    for at in range(peers):
        start = (place_ref[0] ^ at) * height
        for copy in mat_copies[at]:
            copy.wait()
        angle_copies[at].wait()

        def diffract(block, at=at, start=start):
            within = block * BLOCK
            rights = []
            for order in range(3):
                rows = pl.ds(height + start + within + (order - 1) * shift, BLOCK)
                rights.append(jnp.concatenate([padded[0, rows], padded[1, rows]], axis=1).astype(BF16))
            got = dot(held_mats[at, block], jnp.concatenate(rights, axis=0))
            real = got[:BLOCK, :width] - got[BLOCK:, width:]
            imag = got[:BLOCK, width:] + got[BLOCK:, :width]
            cosine, sine = cos_sin(held_angles[at, aligned(within, BLOCK)].astype(F32) * (1.0 / ANGLE_STEPS))
            rows = aligned(start + within, BLOCK)
            wave[0, rows] = real * cosine - imag * sine
            wave[1, rows] = real * sine + imag * cosine

        loop(own_blocks, diffract, 4)

    def mix(at):
        parts = []
        for half in range(2):
            down = at * 16 + half * 8
            values = [
                (wave[0, aligned(one * part + down, 8)], wave[1, aligned(one * part + down, 8)])
                for one in range(RADIX)
            ]
            parts.append(butterfly(values, 1))
        for one in range(RADIX):
            real, imag = (jnp.concatenate([parts[0][one][c], parts[1][one][c]], axis=0) for c in range(2))
            mixed[one, aligned(at * 16, 16)] = jnp.concatenate([real, imag], axis=1).astype(BF16)

    loop(part // 16, mix, 2)
    for group in range(cols_at):
        table_copies[group].wait()

        def fold(first, group=group):
            at = group * firsts + first
            got = dot(held_tables[0][at], mixed[at])
            real = (got[:part, :width] - got[part:, width:]).astype(BF16)
            imag = (got[:part, width:] + got[part:, :width]).astype(BF16)
            held_out[:, group, first, 0] = real.reshape(rows_at, seconds, width)
            held_out[:, group, first, 1] = imag.reshape(rows_at, seconds, width)

        loop(firsts, fold, firsts)
        fetch(held_out.at[:, group], out_ref.at[:, group])
    for copy in copies[-cols_at:]:
        copy.wait()


def column_work(later, place, shift, current, mats, angles, tables, col_count):
    peers = len(mats)
    height, width = angles[0].shape
    extent = height * peers
    part = extent // RADIX
    groups = [[current] if later else current, *mats, angles, tables if later else tables[:1]]
    counts = [len(group) for group in groups]
    sent = jax.ShapeDtypeStruct((peers, col_count, RADIX // col_count, 2, part // peers, width), BF16)
    held = sent.shape if later else (peers, 2, height, width)
    copies = sum(counts[1:-2]) + peers + (4 if later else 2) * col_count + peers

    def body(*refs):
        column_body(later, peers, counts, *refs)

    smem, anywhere = pl.BlockSpec(memory_space=pltpu.SMEM), pl.BlockSpec(memory_space=pl.ANY)
    return pl.pallas_call(
        body,
        out_shape=sent,
        in_specs=[smem, smem] + [anywhere] * sum(counts),
        out_specs=anywhere,
        scratch_shapes=[
            pltpu.VMEM((2, extent + 2 * height, width), F32),
            pltpu.VMEM((2, extent, width), F32),
            pltpu.VMEM((RADIX, part, 2 * width), BF16),
            pltpu.VMEM(held, BF16),
            pltpu.VMEM((peers, height // BLOCK, 2 * BLOCK, 3 * BLOCK), BF16),
            pltpu.VMEM((peers, height, width), angles[0].dtype),
            pltpu.VMEM(sent.shape, BF16),
            *[pltpu.VMEM(table.shape, BF16) for table in groups[-1]],
            pltpu.SemaphoreType.DMA((copies,)),
        ],
        compiler_params=params(),
        name="column_later" if later else "column_first",
    )(place, shift, *[one for group in groups for one in group])


def row_mix(order, in_ref, turn_ref, mixed, arrived):
    blocks, firsts, _, seconds, lanes = in_ref.shape
    radix, _, _, part = mixed.shape
    tiles = part // lanes

    def one_first(first):
        for tile in range(tiles):
            across = pl.ds(tile * lanes, lanes)
            for at in range(0, seconds, 16):
                values = [
                    (
                        in_ref[order[one * tiles + tile], first, 0, pl.ds(at, 16)].astype(F32),
                        in_ref[order[one * tiles + tile], first, 1, pl.ds(at, 16)].astype(F32),
                    )
                    for one in range(radix)
                ]
                for one, (real, imag) in enumerate(butterfly(values, 1)):
                    cosine, sine = turn_ref[one, 0, :, across], turn_ref[one, 1, :, across]
                    down = first * seconds + at
                    mixed[one, 0, pl.ds(down, 16), across] = (real * cosine - imag * sine).astype(BF16)
                    mixed[one, 1, pl.ds(down, 16), across] = (real * sine + imag * cosine).astype(BF16)

    for first in range(firsts):
        arrived(first)
        one_first(first)


def core_dot(left, tile_ref, sign):
    count, _, rows, depth = left.shape
    lanes = tile_ref.shape[1] // 2
    got = dot(left.reshape(count * 2 * rows, depth), tile_ref).reshape(count, 2, rows, 2 * lanes)
    first, second = got[:, 0], got[:, 1]
    if sign > 0:
        return first[..., :lanes] - second[..., lanes:], second[..., :lanes] + first[..., lanes:]
    return first[..., :lanes] + second[..., lanes:], second[..., :lanes] - first[..., lanes:]


def row_body(order, in_any, mask_any, core_any, turn_ref, out_any, mixed, passed, back, in_ref, mask_ref, core_ref, out_ref, sems):
    blocks, firsts, _, seconds, lanes = in_ref.shape
    copies = [pltpu.make_async_copy(in_any.at[:, one], in_ref.at[:, one], sems.at[one]) for one in range(firsts)]
    copies.append(pltpu.make_async_copy(core_any, core_ref, sems.at[firsts]))
    copies.append(pltpu.make_async_copy(mask_any, mask_ref, sems.at[firsts + 1]))
    for copy in copies:
        copy.start()
    radix, _, _, part = mixed.shape
    tiles = part // lanes
    rows = firsts * seconds
    row_mix(order, in_ref, turn_ref, mixed, lambda first: copies[first].wait())
    at_once = min(GROUP, radix)
    copies[firsts].wait()
    copies[firsts + 1].wait()

    for group in range(0, radix, at_once):
        these = pl.ds(group, at_once)

        def forward(tile, these=these):
            real, imag = core_dot(mixed[these], core_ref[tile], 1)
            kept = mask_ref[tile, these].astype(F32)
            across = aligned(tile * lanes, lanes)
            passed[these, 0, :, across] = (real * kept).astype(BF16)
            passed[these, 1, :, across] = (imag * kept).astype(BF16)

        loop(tiles, forward, tiles)

        def backward(tile, these=these):
            real, imag = core_dot(passed[these], core_ref[tile], -1)
            across = aligned(tile * lanes, lanes)
            cosine, sine = turn_ref[these, 0, :, across], turn_ref[these, 1, :, across]
            back[these, 0, :, across] = real * cosine + imag * sine
            back[these, 1, :, across] = imag * cosine - real * sine

        loop(tiles, backward, tiles)

    def close(first):
        for tile in range(tiles):
            across = pl.ds(tile * lanes, lanes)
            for at in range(0, seconds, 16):
                down = pl.ds(first * seconds + at, 16)
                values = [(back[one, 0, down, across], back[one, 1, down, across]) for one in range(radix)]
                for one, (real, imag) in enumerate(butterfly(values, -1)):
                    out_ref[order[one * tiles + tile], first, 0, pl.ds(at, 16)] = real.astype(BF16)
                    out_ref[order[one * tiles + tile], first, 1, pl.ds(at, 16)] = imag.astype(BF16)

    back_copies = []
    for first in range(firsts):
        close(first)
        copy = pltpu.make_async_copy(out_ref.at[:, first], out_any.at[:, first], sems.at[firsts + 2 + first])
        copy.start()
        back_copies.append(copy)
    for copy in back_copies:
        copy.wait()


def row_work(order, received, mask, tables):
    blocks, firsts, _, seconds, lanes = received.shape
    core, turns = tables
    radix, part = turns.shape[0], core.shape[1]
    rows = firsts * seconds

    anywhere = pl.BlockSpec(memory_space=pl.ANY)

    def body(*refs):
        row_body(order, *refs)

    return pl.pallas_call(
        body,
        out_shape=jax.ShapeDtypeStruct(received.shape, BF16),
        in_specs=[anywhere, anywhere, anywhere, vmem(1)[0]],
        out_specs=anywhere,
        scratch_shapes=[
            pltpu.VMEM((radix, 2, rows, part), BF16),
            pltpu.VMEM((radix, 2, rows, part), BF16),
            pltpu.VMEM((radix, 2, rows, part), F32),
            *[pltpu.VMEM(one.shape, BF16) for one in (received, mask, core, received)],
            pltpu.SemaphoreType.DMA((2 * firsts + 2,)),
        ],
        compiler_params=params(),
        name="row_both",
    )(received, mask, core, turns)


def last_row_body(order, number, place_ref, in_any, core_any, turn_ref, *refs):
    outs, (mixed, in_ref, core_ref, sems) = refs[:-4], refs[-4:]
    firsts, seconds = in_ref.shape[1], in_ref.shape[3]
    these = pl.ds(number * seconds, seconds)
    copies = [
        pltpu.make_async_copy(in_any.at[:, one, :, these], in_ref.at[:, one], sems.at[one]) for one in range(firsts)
    ]
    copies.append(pltpu.make_async_copy(core_any, core_ref, sems.at[firsts]))
    for copy in copies:
        copy.start()
    radix = mixed.shape[0]
    at_once = min(GROUP, radix)
    row_mix(order, in_ref, turn_ref, mixed, lambda first: copies[first].wait())
    copies[firsts].wait()
    for group in range(0, radix, at_once):
        these = pl.ds(group, at_once)
        for distance, out_ref in enumerate(outs):
            real, imag = core_dot(mixed[these], core_ref[place_ref[0] ^ distance], 1)
            out_ref[0, these] = real.astype(BF16)
            out_ref[1, these] = imag.astype(BF16)


def last_row_work(order, place, received, tables, number, chunks):
    blocks, firsts, _, seconds, lanes = received.shape
    core, turns = tables
    radix, part = turns.shape[0], core.shape[1]
    seconds //= chunks
    rows = firsts * seconds

    def body(*refs):
        last_row_body(order, number, *refs)

    def whole(array):
        return pl.BlockSpec(array.shape, lambda i: (0,) * array.ndim)

    anywhere = pl.BlockSpec(memory_space=pl.ANY)
    sent = jax.ShapeDtypeStruct((2, radix, rows, lanes), BF16)
    return pl.pallas_call(
        body,
        grid=(1,),
        out_shape=[sent] * (part // lanes),
        in_specs=[pl.BlockSpec(memory_space=pltpu.SMEM), anywhere, anywhere, whole(turns)],
        out_specs=[whole(sent)] * (part // lanes),
        scratch_shapes=[
            pltpu.VMEM((radix, 2, rows, part), BF16),
            pltpu.VMEM((blocks, firsts, 2, seconds, lanes), BF16),
            pltpu.VMEM(core.shape, BF16),
            pltpu.SemaphoreType.DMA((firsts + 1,)),
        ],
        compiler_params=params(),
        cost_estimate=pl.CostEstimate(flops=8 * rows * part * part * radix, bytes_accessed=2**22, transcendentals=0),
        name="row_last",
    )(place, received, core, turns)


def mask_body(in_ref, down_ref, across_ref, out_ref):
    groups, radix, rows, lanes = out_ref.shape
    turned = dot(down_ref[...], in_ref[...].astype(BF16)).astype(BF16)
    for tile in range(0, radix * lanes, 256):
        got = dot(turned, across_ref[:, tile : tile + 256]).astype(BF16)
        for within in range(0, 256, lanes):
            out_ref[:, (tile + within) // lanes] = got[:, within : within + lanes].reshape(groups, rows, lanes)


def mask_work(transmission, row_count, col_count, radix):
    height, width = transmission.shape
    down = regroup(height, RADIX).T
    across = regroup(width, radix)
    return pl.pallas_call(
        mask_body,
        out_shape=jax.ShapeDtypeStruct((col_count, radix, height // col_count, width // radix), BF16),
        in_specs=vmem(3),
        out_specs=vmem(1)[0],
        compiler_params=params(),
        name="mask_order",
    )(transmission, jnp.asarray(down), jnp.asarray(across))


def closing_body(groups, place_ref, *refs):
    given, (keep_ref, down_ref, across_ref), (out_ref, joined, turned) = refs[:groups], refs[groups : groups + 3], refs[-3:]
    _, radix, rows, lanes = given[0].shape
    for distance in range(groups):
        down = aligned((place_ref[0] ^ distance) * rows, rows)
        for number in range(2):
            for at in range(radix):
                joined[number, down, pl.ds(at * lanes, lanes)] = given[distance][number, at]
    for number in range(2):
        turned[number] = dot(down_ref[...], joined[number]).astype(BF16)
        for tile in range(0, radix * lanes, 256):
            across = pl.ds(tile, 256)
            out_ref[number, :, across] = dot(turned[number], across_ref[:, across]) * keep_ref[:, across]


def closing_work(place, received, transmission, earlier, number, chunks):
    groups = len(received)
    _, radix, rows, lanes = received[0].shape
    height, width = transmission.shape
    height //= chunks
    down = jnp.asarray(regroup(height, RADIX))
    across = jnp.asarray(regroup(width, radix).T)

    def body(*refs):
        closing_body(groups, *refs[: groups + 4], *refs[-3:])

    def whole(array):
        return pl.BlockSpec(array.shape, lambda i: (0,) * array.ndim)

    in_specs = [pl.BlockSpec(memory_space=pltpu.SMEM)] + [whole(one) for one in received]
    in_specs += [pl.BlockSpec((height, width), lambda i: (number, 0)), whole(down), whole(across)]
    arguments = [place, *received, transmission, down, across]
    aliases = {}
    if earlier is not None:
        aliases = {len(arguments): 0}
        in_specs.append(pl.BlockSpec(memory_space=pl.ANY))
        arguments.append(earlier)
    return pl.pallas_call(
        body,
        grid=(1,),
        out_shape=jax.ShapeDtypeStruct((2, height * chunks, width), F32),
        in_specs=in_specs,
        out_specs=pl.BlockSpec((2, height, width), lambda i: (0, number, 0)),
        scratch_shapes=[pltpu.VMEM((2, height, width), BF16), pltpu.VMEM((2, height, width), BF16)],
        input_output_aliases=aliases,
        compiler_params=params(24 * 1024 * 1024),
        cost_estimate=pl.CostEstimate(flops=4 * height * width * width, bytes_accessed=2**22, transcendentals=0),
        name="closing_order",
    )(*arguments)


def exchange(value, axis):
    return lax.all_to_all(value, axis, split_axis=0, concat_axis=0, tiled=True)


def swap(value, axis, distance):
    if distance == 0:
        return value
    return lax.ppermute(value, axis, [(at, at ^ distance) for at in range(lax.axis_size(axis))])


def widen(value):
    short = -value.shape[-1] % LANES
    return jnp.pad(value, [(0, 0)] * (value.ndim - 1) + [(0, short)]) if short else value


def after(value, earlier):
    return lax.optimization_barrier((value, earlier))[0]


def gather_mats(mats):
    peers = lax.axis_size("rows")
    if peers != 8:
        result = [[swap(mats, "rows", distance)] for distance in range(peers)]
        return result, result[1]
    half = mats.shape[0] // 2
    by_x, by_y = swap(mats, "rows", 2), swap(mats, "rows", 4)
    across = [swap(by_x[:half], "rows", 4), swap(by_y[half:], "rows", 2)]
    result = []
    for pieces in ([mats], [by_x], [by_y], across):
        result += [pieces, [swap(piece, "rows", 1) for piece in pieces]]
    return result, (by_x, by_y)


def spread(value, width):
    peers, along = lax.axis_size("rows"), lax.axis_index("rows")
    chips = []
    for distance in range(0, peers, 2):
        start = ((along ^ distance) // 2) * (2 * width)
        piece = lax.dynamic_slice_in_dim(value, start, 2 * width, value.ndim - 1)
        chips.append(swap(piece, "rows", distance))

    def part(piece, core):
        return lax.dynamic_slice_in_dim(piece, core * width, width, value.ndim - 1)

    core = along % 2
    other = swap(jnp.stack([part(piece, 1 - core) for piece in chips]), "rows", 1)
    return [widen(part(piece, core)) for piece in chips] + [widen(other)]


def on_device(spectrum, diffraction, order_mask, phases, transmission, shifts):
    height, wide = spectrum.shape[1:]
    row_count, col_count = lax.axis_size("rows"), lax.axis_size("cols")
    devices = row_count * col_count
    full_rows, full_cols = height * row_count, wide * col_count
    width = wide // row_count
    part = LANES * col_count
    radix = full_cols // part
    forward, backward = column_tables(full_rows)
    column_all = (jnp.asarray(forward), jnp.asarray(backward))
    core, turns = row_tables(full_cols, part)
    row_all = (jnp.asarray(core), jnp.asarray(turns))

    along, above = lax.axis_index("rows"), lax.axis_index("cols")
    place_rows, place_cols = (at.astype(jnp.int32).reshape(1) for at in (along, above))

    masked = diffraction * order_mask.astype(BF16)[None, :, :, None, None]
    blocks = height // BLOCK
    masked = masked.transpose(1, 0, 3, 2, 4).reshape(blocks, 2 * BLOCK, 3 * BLOCK)
    mats, first_mats = gather_mats(masked)
    current = spread(spectrum, width)
    codes = jnp.round(phases * ANGLE_STEPS).astype(jnp.int16)
    angles = [spread(codes[0], width), spread(codes[1], width)]
    kept = exchange(mask_work(transmission, row_count, col_count, radix), "cols")

    narrow = width < LANES
    tiles = full_cols // LANES
    if narrow:
        order = list(range(tiles))
    else:
        order = [(at % row_count) * col_count + at // row_count for at in range(tiles)]

    def to_rows(value):
        got = exchange(value[..., :width].reshape(devices, *value.shape[2:-1], width), ("rows", "cols"))
        if not narrow:
            return got
        joined = LANES // width
        got = got.reshape(row_count, col_count, *got.shape[1:]).swapaxes(0, 1).reshape(tiles, joined, *got.shape[1:])
        return jnp.moveaxis(got, 1, -2).reshape(tiles, *got.shape[2:-1], LANES)

    def to_columns(value):
        if narrow:
            joined = LANES // width
            value = jnp.moveaxis(value.reshape(*value.shape[:-1], joined, width), -2, 1)
            value = value.reshape(col_count, row_count, *value.shape[2:]).swapaxes(0, 1)
            value = value.reshape(devices, *value.shape[2:])
        got = exchange(value, ("rows", "cols"))
        return widen(got.reshape(row_count, col_count, *got.shape[1:]))

    for bounce in range(BOUNCES):
        sent = column_work(
            bounce > 0, place_rows, shifts[bounce : bounce + 1], current, mats, angles[bounce], column_all, col_count
        )
        received = to_rows(sent)
        if bounce < BOUNCES - 1:
            current = to_columns(row_work(order, received, kept, row_all))
    chunks = 2 if received.shape[3] % 32 == 0 else 1
    worked = [last_row_work(order, place_cols, received, row_all, number, chunks) for number in range(chunks)]
    worked = [[swap(one, "cols", distance) for distance, one in enumerate(chunk)] for chunk in worked]
    outgoing = None
    for number in range(chunks):
        outgoing = closing_work(place_cols, worked[number], transmission, outgoing, number, chunks)
    return outgoing


def solution(mesh):
    placed = (
        P(None, "rows", "cols"),
        P(None, "rows", None, None, None),
        P("rows", None),
        P(None, "rows", "cols"),
        P("rows", "cols"),
        P(),
    )
    return jax.shard_map(
        on_device, mesh=mesh, in_specs=placed, out_specs=P(None, "rows", "cols"), check_vma=False
    )
```
